512 devices in a mesh: src: 16 (over z, core), tm: 32 (over x, y).
Axes of the slice: x: 4, y: 8, z: 8, core: 2. Of those that a mesh axis runs over, the one named last changes fastest.
Arguments:
- greens: bfloat16 [65536, 12288], P('tm', 'src')
- pairs: int32 [16, 2], P('src'), may hold values from 0 to 15, as said below
- onsets: int32 [16], replicated, may hold values from 0 to 32767
Outputs:
- gram: float32 [16, 768, 768], P('src', 'tm')
The draws below stay inside these ranges and needn't reach their ends.
Inputs may be any that keep to these rules, and one draw needn't show every extreme that they name: `pairs`: row s names the blocks s and (s - 1) mod 16, in either order.
All inputs are finite; a program needn't handle non-finite values.
Results may differ from the reference program's by a relative error of at most 0.0003.
Values may be sent and summed in bfloat16 or wider, within the bound.
A program may use at most 64 MiB of HBM per device.

```python
import jax
import jax.numpy as jnp
from jax import lax

SRC_BLK = 768
BLOCKS = 16
ROWS = 65536


def draw_greens(key, part):
    factors = 16
    base_key = jax.random.fold_in(key, 11)
    keys = jax.random.split(base_key, 4)
    basis = jax.random.normal(keys[0], (ROWS, factors), jnp.float32)
    centres = jax.random.uniform(keys[1], (factors,), jnp.float32) * ROWS
    row_pos = jnp.arange(ROWS, dtype=jnp.float32)
    envelope = jnp.exp(-((row_pos[:, None] - centres[None, :]) / (0.3 * ROWS)) ** 2)
    rising = 1.0 + 0.8 * row_pos / ROWS
    shaped = basis * envelope

    def one_block(index):
        block_key = jax.random.fold_in(keys[3], index)
        mix_key, noise_key = jax.random.split(block_key, 2)
        mix = jax.random.normal(mix_key, (factors, SRC_BLK), jnp.float32) * 0.35
        noise = jax.random.normal(noise_key, (ROWS, SRC_BLK), jnp.float32)
        values = jnp.dot(shaped, mix, precision=lax.Precision.HIGHEST) + noise
        values = values * rising[:, None] * 0.6
        return values.astype(jnp.bfloat16)
    blocks = lax.map(one_block, jnp.arange(BLOCKS, dtype=jnp.int32))
    return jnp.moveaxis(blocks, 0, 1).reshape(ROWS, BLOCKS * SRC_BLK)


def draw_pairs(key, part):
    owners = jnp.arange(BLOCKS, dtype=jnp.int32)
    before = (owners + BLOCKS - 1) % BLOCKS
    flips = jax.random.randint(jax.random.fold_in(key, 23), (BLOCKS,), 0, 2, dtype=jnp.int32)
    first = jnp.where(flips == 1, owners, before)
    second = jnp.where(flips == 1, before, owners)
    return jnp.stack([first, second], axis=1).astype(jnp.int32)


def with_ends(values, own_key, least, high):
    longest = values.shape.index(max(values.shape))
    spots = []
    for shift in (0, 1):
        where = [jax.random.randint(jax.random.fold_in(own_key, axis), (), 0, length) for axis, length in enumerate(values.shape)]
        where[longest] = (where[longest] + shift) % values.shape[longest]
        spots.append(tuple(where))
    return values.at[spots[0]].set(least).at[spots[1]].set(high)


def setup_inputs(seed: int = 0) -> dict:
    streams_of = jax.random.split(jax.random.key(seed), 4)
    greens = draw_greens(jax.random.fold_in(streams_of[3], 71), 0)
    pairs = draw_pairs(jax.random.fold_in(streams_of[3], 71), 0)
    onsets = with_ends(jax.random.randint(streams_of[2], (BLOCKS,), 0, ROWS // 2), jax.random.fold_in(streams_of[2], 1), 0, (ROWS // 2) - 1).astype(jnp.int32)
    return dict(greens=greens, pairs=pairs, onsets=onsets)


def masked_block(greens, block, onset):
    piece = lax.dynamic_slice(greens, (jnp.int32(0), (block * SRC_BLK).astype(jnp.int32)), (ROWS, SRC_BLK))
    row_ids = jnp.arange(ROWS, dtype=jnp.int32)
    return jnp.where((row_ids >= onset)[:, None], piece, jnp.zeros_like(piece))

def reference(greens, pairs, onsets):

    def one_tile(pair):
        first = pair[0]
        second = pair[1]
        left = masked_block(greens, first, onsets[first])
        right = masked_block(greens, second, onsets[second])
        left_f = left.astype(jnp.float32)
        right_f = right.astype(jnp.float32)
        norm_left = lax.optimization_barrier(jnp.sum(left_f * left_f, axis=0))
        norm_right = lax.optimization_barrier(jnp.sum(right_f * right_f, axis=0))
        product = lax.dot_general(left, right, (((0,), (0,)), ((), ())), preferred_element_type=jnp.float32)
        return product * lax.rsqrt(norm_left + 1e-06)[:, None] * lax.rsqrt(norm_right + 1e-06)[None, :]
    return lax.map(one_tile, pairs)
```

```python
import functools

import jax
import jax.numpy as jnp
from jax import lax
from jax.experimental import pallas as pl
from jax.experimental.pallas import tpu as pltpu
from jax.sharding import Mesh
from jax.sharding import PartitionSpec as P

MESH = pl.DeviceIdType.MESH
F32 = jnp.float32
BF16 = jnp.bfloat16
NZ, NX, NY = 8, 4, 8
LAG0 = 4
LAG1 = 1


def remote(src, dst, send, recv, **where):
    return pltpu.make_async_remote_copy(
        src_ref=src, dst_ref=dst, send_sem=send, recv_sem=recv, device_id=where, device_id_type=MESH
    )


def kernel(
    greens, pairs, onsets, out,
    held, nat, sent, got, shift, tbuf, nbuf, units, rx_half, rx_full, ry_half, ry_full,
    wide, w_half, w_full, res, res_c, npart, nx_got, ny_got, scale, flag, flag_c,
    load_sem, raw_send, raw_recv, z_send, z_recv, core_send, ring_send, ring_recv,
    res_send, res_recv, n_send, n_recv, f_send, f_recv,
):
    z, c, x, y = (lax.axis_index(a) for a in ("z", "c", "x", "y"))
    rows, width = greens.shape
    half = rows // 2
    cols = width // 3
    t = x * NY + y
    row_start = t * rows
    z_up, z_down = lax.rem(z + 1, NZ), lax.rem(z + NZ - 1, NZ)
    own = 2 * z + c
    low = lax.rem(own + 2 * NZ - 1, 2 * NZ)
    high = lax.rem(own + 1, 2 * NZ)

    def at_x(d):
        return lax.rem(x + d + NX, NX)

    def at_y(d):
        return lax.rem(y + d + NY, NY)

    bar = pltpu.get_barrier_semaphore()

    def hello(**where):
        pl.semaphore_signal(bar, inc=1, device_id=where, device_id_type=MESH)

    loads = [
        pltpu.make_async_copy(
            greens.at[pl.ds(i * 512, 512)], held.at[pl.ds(i * 512, 512)], load_sem.at[i]
        )
        for i in range(rows // 512)
    ]
    for i in (2, 3, 0, 1):
        pl.when(c == 0)(loads[i].start)
    for i in (0, 1, 2, 3):
        pl.when(c == 1)(loads[i].start)
    for d in range(1, NX):
        hello(x=at_x(d))
    for d in range(1, NY):
        hello(y=at_y(d))
    hello(c=1 - c)

    @pl.when(c == 0)
    def _():
        hello(z=z_up)
        hello(z=z_down)
        hello(z=z_down, c=1)

    @pl.when(c == 1)
    def _():
        hello(z=z_up, c=0)

    for k in range(3):
        i = lax.broadcasted_iota(jnp.int32, (cols, width), 0)
        j = lax.broadcasted_iota(jnp.int32, (cols, width), 1)
        hit = j == i + 16 * lax.shift_right_logical(i, 3) + 8 * k
        shift[k] = jnp.where(hit, F32(1), F32(0)).astype(BF16)

    own_first = pairs[0, 0] == own
    flag[...] = jnp.where(own_first, jnp.ones_like(flag), jnp.zeros_like(flag))

    @pl.when(c == 0)
    def _():
        pl.semaphore_wait(bar, 14)

    @pl.when(c == 1)
    def _():
        pl.semaphore_wait(bar, 12)

    def chunk(k, h):
        for b in range(2):
            part = held[pl.ds(h * half + b * 512, 512), :]
            sent[k, h, :, pl.ds(b * 512, 512)] = lax.dot_general(
                shift[k], part, (((1,), (1,)), ((), ())), preferred_element_type=F32
            ).astype(BF16)

    def masks(nat_rows, nat_onset):
        own_from = onsets[own] - row_start
        nat_from = nat_onset - row_start
        step = 64

        def body(i, total):
            at = pl.multiple_of(i * step, step)
            block = held[pl.ds(at, step), :].astype(F32)
            ids = at + lax.broadcasted_iota(jnp.int32, (step, width), 0)
            mine = jnp.where(ids >= own_from, block, F32(0))

            @pl.when(i < nat_rows // step)
            def _():
                nat[pl.ds(at, step), :] = jnp.where(ids >= nat_from, block, F32(0)).astype(BF16)

            return total + jnp.sum((mine * mine).reshape(step // 8, 8, width), axis=0)

        total = lax.fori_loop(0, rows // step, body, jnp.zeros((8, width), F32))
        npart[0] = jnp.sum(total, axis=0, keepdims=True)

    def mask_c():
        nat_from = jnp.maximum(onsets[high], onsets[lax.rem(own + 2, 2 * NZ)]) - row_start
        step = 64

        @pl.loop(0, half // step)
        def _(i):
            at = pl.multiple_of(half + i * step, step)
            ids = at + lax.broadcasted_iota(jnp.int32, (step, width), 0)
            block = nat[pl.ds(at, step), :].astype(F32)
            nat[pl.ds(at, step), :] = jnp.where(ids >= nat_from, block, F32(0)).astype(BF16)

    nx = [
        remote(npart.at[0], nx_got.at[d - 1], n_send.at[d - 1], n_recv.at[d - 1], x=at_x(d))
        for d in range(1, NX)
    ]
    ny = [
        remote(npart.at[1], ny_got.at[d - 1], n_send.at[2 + d], n_recv.at[2 + d], y=at_y(d))
        for d in range(1, NY)
    ]

    def norm_x():
        for cp in nx:
            cp.start()

    def norm_y():
        total = npart[0]
        for d, cp in enumerate(nx):
            cp.wait_recv()
            total = total + nx_got[d]
        npart[1] = total
        for cp in ny:
            cp.start()

    def norm_end(pass_on):
        total = npart[1]
        for d, cp in enumerate(ny):
            cp.wait_recv()
            total = total + ny_got[d]
        scale[0] = lax.rsqrt(total + F32(1e-6))
        pass_on.start()

    def product(u, k, parts, natural):
        for q in range(3):
            at = pl.ds(q * cols, cols)
            total = None
            for slot, first in parts:
                term = jnp.dot(got[k, slot], nat[pl.ds(first, half), at], preferred_element_type=F32)
                total = term if total is None else total + term
            tbuf[:, at] = total
            nbuf[at, :] = total.T
        for g in range(NX):
            turned = nbuf[pl.ds(192 * g, 192), :].reshape(8, 3, 8, cols)
            for q in range(3):
                at = pl.ds(q * cols, cols)
                plain = tbuf[pl.ds(64 * g, 64), at]
                units[u, g, :, at] = jnp.where(natural, turned[:, q].reshape(64, cols), plain)

    def ring(n, axis, to, group, add, halves, slots, sems, finish):
        deep = n // 2

        def sends(step, lo, hi):
            send, recv, base = sems
            return (
                remote(lo, slots(step, 0), send.at[base + 2 * step], recv.at[base + 2 * step], **{axis: to(1)}),
                remote(hi, slots(step, 1), send.at[base + 2 * step + 1], recv.at[base + 2 * step + 1], **{axis: to(-1)}),
            )

        started = []

        def begin():
            far = group(to(deep))
            pair = sends(0, halves(far, 0), halves(far, 1))
            started.append(pair)
            for cp in pair:
                cp.start()

        def middle(step):
            for side, cp in enumerate(started[-1]):
                cp.wait_recv()
                where = group(to((deep - step) * (1 - 2 * side)))
                add(where, slots(step - 1, side), side if step == 1 else None)
            pair = sends(step, group(to(deep - step)), group(to(step - deep)))
            started.append(pair)
            for cp in pair:
                cp.start()

        def end():
            for cp in started[-1]:
                cp.wait_recv()
            finish(group(to(0))[...] + slots(deep - 1, 0)[...] + slots(deep - 1, 1)[...])

        stages = [begin] + [functools.partial(middle, s) for s in range(1, deep)] + [end]
        return stages, started

    def add_into(halves):
        def add(where, arrived, side):
            where = where if side is None else halves(where, side)
            where[...] = where[...] + arrived[...]

        return add

    def unit_stages(u, x_first, done):
        sems = (ring_send, ring_recv)

        def put(value):
            wide[u, pl.ds(0, 64 if x_first else 32)] = value.reshape(-1, width)

        def put_res(value):
            res[u] = value
            done()

        def half_rows_x(ref, s):
            return ref.at[pl.ds(32 * s, 32)]

        def half_rows_y(ref, s):
            return ref.at[pl.ds(2 * s, 2)]

        def half_cols(ref, s):
            return ref.at[:, pl.ds(s * (width // 2), width // 2)]

        if x_first:
            v = u - 3
            one = ring(
                NX, "x", at_x, lambda g: units.at[u, g], add_into(half_rows_x), half_rows_x,
                lambda step, side: (rx_half.at[v, side] if step == 0 else rx_full.at[v, side]),
                (*sems, 12 * u), put,
            )
            n, axis, to, base = NY, "y", at_y, 12 * u + 4
        else:
            one = ring(
                NY, "y", at_y, lambda g: units.at[u, :, pl.ds(pl.multiple_of(8 * g, 8), 8)],
                add_into(half_rows_y), half_rows_y,
                lambda step, side: (ry_half.at[u, side] if step == 0 else ry_full.at[u, step - 1, side]),
                (*sems, 12 * u), put,
            )
            n, axis, to, base = NX, "x", at_x, 12 * u + 8
        two = ring(
            n, axis, to, lambda g: wide.at[u, pl.ds(pl.multiple_of(8 * g, 8), 8)], add_into(half_cols), half_cols,
            lambda step, side: (w_half.at[u, side] if step == 0 else w_full.at[u, step - 1, side]),
            (*sems, base), put_res,
        )
        a, b = one[0], two[0]

        def joint():
            a[-1]()
            b[0]()

        return a[:-1] + [joint] + b[1:], (one[1], two[1])

    def finish_tile(direct, turned):
        total = None
        for k in range(3):
            out[0, pl.ds(8 * k, 8), :] = direct(k)
            piece = turned(k)
            piece = jnp.concatenate([piece[:, q * cols : (q + 1) * cols] for q in range(3)], axis=0)
            top = piece.astype(BF16).astype(F32)
            rest = piece - top
            mid = rest.astype(BF16).astype(F32)
            stack = jnp.concatenate([top, mid, rest - mid], axis=0).astype(BF16)
            term = jnp.dot(stack, shift[k], preferred_element_type=F32)
            total = term if total is None else total + term
        value = out[0] + (total[:24] + total[24:48] + total[48:])
        mine, other = scale[0], scale[1]
        left = jnp.where(own_first, mine, other)
        right = jnp.where(own_first, other, mine)
        i = lax.broadcasted_iota(jnp.int32, (24, width), 0)
        j = lax.broadcasted_iota(jnp.int32, (24, width), 1)
        down = jnp.sum(jnp.where(j == i + 24 * t, left, F32(0)), axis=1, keepdims=True)
        out[0] = value * down * right

    def wait_sends(groups, others):
        for one, two in groups:
            for pair in one + two:
                for cp in pair:
                    cp.wait_send()
        for cp in nx + ny + others:
            cp.wait_send()

    raw = remote(greens.at[pl.ds(half, half)], nat.at[pl.ds(half, half)], raw_send, raw_recv, c=0)

    @pl.when(c == 0)
    def _():
        flags = remote(flag, flag_c, f_send, f_recv, z=z_down)
        flags.start()
        to_c = [remote(sent.at[k, 1], got.at[k, 1], z_send.at[k], z_recv.at[k, 1], z=z_down) for k in range(3)]
        to_a = [
            [remote(sent.at[k, h], got.at[k, h], core_send.at[k, h], z_recv.at[k, h], c=1) for h in range(2)]
            for k in range(3)
        ]
        for i in (2, 3):
            loads[i].wait()
        for k in range(3):
            chunk(k, 1)
            to_c[k].start()
            to_a[k][1].start()
            if k == 0:
                for i in (0, 1):
                    loads[i].wait()
            chunk(k, 0)
            to_a[k][0].start()
        masks(half, jnp.maximum(onsets[own], onsets[low]))
        norm_x()
        raw.wait_recv()
        mask_c()
        passed = remote(scale.at[0], scale.at[1], n_send.at[10], n_recv.at[10], c=1)
        flags.wait_recv()
        natural_c = jnp.broadcast_to(flag_c[0:1, 0:1] < F32(0.5), (64, cols))
        res_out = [remote(res.at[3 + k], res_c.at[k], res_send.at[k], res_recv.at[k], z=z_up) for k in range(3)]

        def nothing():
            pass

        plan = []
        groups = []
        for k in range(3):
            stages, started = unit_stages(k, False, nothing)
            plan.append((LAG0 * k, k, 0, stages))
            groups.append(started)
            stages, started = unit_stages(3 + k, True, res_out[k].start)
            plan.append((LAG0 * k, k, 1, stages))
            groups.append(started)
        for slot in range(2 * LAG0 + 7):
            for start, k, kind, stages in plan:
                if start == slot:
                    if kind == 0:
                        pltpu.make_async_copy(got.at[k, 0], got.at[k, 0], z_recv.at[k, 0]).wait()
                        product(k, k, ((0, 0),), own_first)
                    else:
                        pltpu.make_async_copy(got.at[k, 1], got.at[k, 1], z_recv.at[k, 1]).wait()
                        product(3 + k, k, ((1, half),), natural_c)
                if 0 <= slot - start < 7:
                    stages[slot - start]()
            if slot == 0:
                norm_y()
            if slot == 2:
                norm_end(passed)
        pltpu.make_async_copy(scale.at[1], scale.at[1], n_recv.at[10]).wait()
        for cp in res_out:
            cp.wait_recv()
        finish_tile(
            lambda k: jnp.where(own_first, res_c[k], res[k]), lambda k: jnp.where(own_first, res[k], res_c[k])
        )
        wait_sends(groups, [flags, passed] + to_c + to_a[0] + to_a[1] + to_a[2] + res_out)

    @pl.when(c == 1)
    def _():
        raw.start()
        to_b = [remote(sent.at[k, 0], got.at[k, 0], z_send.at[k], z_recv.at[k, 0], z=z_up, c=0) for k in range(3)]
        for i in (0, 1):
            loads[i].wait()
        for k in range(3):
            chunk(k, 0)
            to_b[k].start()
        for i in (2, 3):
            loads[i].wait()
        masks(rows, jnp.maximum(onsets[own], onsets[low]))
        norm_x()
        passed = remote(scale.at[0], scale.at[1], n_send.at[10], n_recv.at[10], z=z_up, c=0)

        def nothing():
            pass

        plan = []
        groups = []
        for k in range(3):
            stages, started = unit_stages(3 + k, True, nothing)
            plan.append((LAG1 * k, k, stages))
            groups.append(started)
        for slot in range(2 * LAG1 + 7):
            for start, k, stages in plan:
                if start == slot:
                    for h in range(2):
                        pltpu.make_async_copy(got.at[k, h], got.at[k, h], z_recv.at[k, h]).wait()
                    product(3 + k, k, ((0, 0), (1, half)), own_first)
                if 0 <= slot - start < 7:
                    stages[slot - start]()
            if slot == 1:
                norm_y()
            if slot == 3:
                norm_end(passed)
        pltpu.make_async_copy(scale.at[1], scale.at[1], n_recv.at[10]).wait()
        finish_tile(
            lambda k: jnp.where(own_first, F32(0), res[3 + k]), lambda k: jnp.where(own_first, res[3 + k], F32(0))
        )
        wait_sends(groups, [raw, passed] + to_b)


def on_device(greens, pairs, onsets):
    rows, width = greens.shape
    half, cols = rows // 2, width // 3
    vmem = pltpu.VMEM
    dma = pltpu.SemaphoreType.DMA
    return pl.pallas_call(
        kernel,
        out_shape=jax.ShapeDtypeStruct((1, width // (NX * NY), width), F32),
        in_specs=[
            pl.BlockSpec(memory_space=pl.ANY),
            pl.BlockSpec(memory_space=pltpu.SMEM),
            pl.BlockSpec(memory_space=pltpu.SMEM),
        ],
        out_specs=pl.BlockSpec(memory_space=vmem),
        scratch_shapes=[
            vmem((rows, width), BF16),
            vmem((rows, width), BF16),
            vmem((3, 2, cols, half), BF16),
            vmem((3, 2, cols, half), BF16),
            vmem((3, cols, width), BF16),
            vmem((cols, width), F32),
            vmem((width, cols), F32),
            vmem((6, NX, 64, width), F32),
            vmem((3, 2, 32, width), F32),
            vmem((3, 2, 64, width), F32),
            vmem((3, 2, 2, 8, width), F32),
            vmem((3, 3, 2, 4, 8, width), F32),
            vmem((6, 64, width), F32),
            vmem((6, 2, 8, width // 2), F32),
            vmem((6, 3, 2, 8, width), F32),
            vmem((6, 8, width), F32),
            vmem((3, 8, width), F32),
            vmem((2, 1, width), F32),
            vmem((NX - 1, 1, width), F32),
            vmem((NY - 1, 1, width), F32),
            vmem((2, 1, width), F32),
            vmem((8, 128), F32),
            vmem((8, 128), F32),
            dma((4,)),
            dma,
            dma,
            dma((3,)),
            dma((3, 2)),
            dma((3, 2)),
            dma((72,)),
            dma((72,)),
            dma((3,)),
            dma((3,)),
            dma((11,)),
            dma((11,)),
            dma,
            dma,
        ],
        compiler_params=pltpu.CompilerParams(
            collective_id=0, has_side_effects=True, vmem_limit_bytes=56 * 1024 * 1024
        ),
        cost_estimate=pl.CostEstimate(flops=5_000_000_000, bytes_accessed=4_000_000, transcendentals=768),
    )(greens, pairs, onsets)


def solution(mesh):
    split = Mesh(mesh.devices.reshape(NZ, 2, NX, NY), ("z", "c", "x", "y"))
    in_specs = (P(("x", "y"), ("z", "c")), P(("z", "c"), None), P())
    out_specs = P(("z", "c"), ("x", "y"), None)
    return jax.shard_map(on_device, mesh=split, in_specs=in_specs, out_specs=out_specs, check_vma=False)
```

```python
import functools

import jax
import jax.numpy as jnp
from jax import lax
from jax.experimental import pallas as pl
from jax.experimental.pallas import tpu as pltpu
from jax.sharding import Mesh
from jax.sharding import PartitionSpec as P

MESH = pl.DeviceIdType.MESH
F32 = jnp.float32
BF16 = jnp.bfloat16
NZ, NX, NY = 8, 4, 8


def remote(src, dst, send, recv, **where):
    return pltpu.make_async_remote_copy(
        src_ref=src, dst_ref=dst, send_sem=send, recv_sem=recv, device_id=where, device_id_type=MESH
    )


def kernel(
    greens, pairs, onsets, out,
    held, nat, nat_c, sent, got, got_c, shift, tbuf, nbuf, units, rx_got, ry_half, ry_full,
    wide, w_got, res, npart, nx_got, ny_got, scale, flag, flag_c,
    load_sem, z_send, z_recv, core_send, a_recv, sum_send, sum_recv, own_recv,
    n_send, n_recv, f_send, f_recv,
):
    z, c, x, y = (lax.axis_index(a) for a in ("z", "c", "x", "y"))
    rows, width = greens.shape
    half = rows // 2
    cols = width // 3
    t = x * NY + y
    row_start = t * rows
    z_up, z_down = lax.rem(z + 1, NZ), lax.rem(z + NZ - 1, NZ)
    own = 2 * z + c
    low = lax.rem(own + 2 * NZ - 1, 2 * NZ)
    high = lax.rem(own + 1, 2 * NZ)

    def at_x(d):
        return lax.rem(x + d + NX, NX)

    def at_y(d):
        return lax.rem(y + d + NY, NY)

    bar = pltpu.get_barrier_semaphore()

    def hello(**where):
        pl.semaphore_signal(bar, inc=1, device_id=where, device_id_type=MESH)

    loads = [
        pltpu.make_async_copy(
            greens.at[pl.ds(i * 512, 512)], held.at[pl.ds(i * 512, 512)], load_sem.at[i]
        )
        for i in range(rows // 512)
    ]
    for i in (2, 3, 0, 1):
        pl.when(c == 0)(loads[i].start)
    for i in (0, 1, 2, 3):
        pl.when(c == 1)(loads[i].start)
    hello(c=1 - c)

    @pl.when(c == 0)
    def _():
        hello(z=z_down, c=1)
        for d in range(NY):
            if d:
                hello(z=z_down, y=at_y(d), c=1)

    @pl.when(c == 1)
    def _():
        hello(z=z_up, c=0)
        for d in range(NY):
            if d:
                hello(z=z_up, y=at_y(d), c=0)

    for d in range(1, NX):
        hello(x=at_x(d))
    for d in range(1, NY):
        hello(y=at_y(d))

    for k in range(3):
        i = lax.broadcasted_iota(jnp.int32, (cols, width), 0)
        j = lax.broadcasted_iota(jnp.int32, (cols, width), 1)
        hit = j == i + 16 * lax.shift_right_logical(i, 3) + 8 * k
        shift[k] = jnp.where(hit, F32(1), F32(0)).astype(BF16)

    own_first = pairs[0, 0] == own
    flag[...] = jnp.where(own_first, jnp.ones_like(flag), jnp.zeros_like(flag))

    def chunk(k, h):
        for b in range(2):
            part = held[pl.ds(h * half + b * 512, 512), :]
            sent[k, h, :, pl.ds(b * 512, 512)] = lax.dot_general(
                shift[k], part, (((1,), (1,)), ((), ())), preferred_element_type=F32
            ).astype(BF16)

    def masks(first, last, targets, total):
        own_from = onsets[own] - row_start
        step = 64

        def body(i, total):
            at = pl.multiple_of(i * step, step)
            block = held[pl.ds(at, step), :].astype(F32)
            ids = at + lax.broadcasted_iota(jnp.int32, (step, width), 0)
            for ref, shifted, onset in targets:
                to = pl.multiple_of(at - shifted, step)
                ref[pl.ds(to, step), :] = jnp.where(ids >= onset - row_start, block, F32(0)).astype(BF16)
            mine = jnp.where(ids >= own_from, block, F32(0))
            return total + jnp.sum((mine * mine).reshape(step // 8, 8, width), axis=0)

        return lax.fori_loop(first // step, last // step, body, total)

    nx = [
        remote(npart.at[0], nx_got.at[d - 1], n_send.at[d - 1], n_recv.at[d - 1], x=at_x(d))
        for d in range(1, NX)
    ]
    ny = [
        remote(npart.at[1], ny_got.at[d - 1], n_send.at[2 + d], n_recv.at[2 + d], y=at_y(d))
        for d in range(1, NY)
    ]

    def norm_x(total):
        npart[0] = jnp.sum(total, axis=0, keepdims=True)
        for cp in nx:
            cp.start()

    def norm_y():
        total = npart[0]
        for d, cp in enumerate(nx):
            cp.wait_recv()
            total = total + nx_got[d]
        npart[1] = total
        for cp in ny:
            cp.start()

    def norm_end(pass_on):
        total = npart[1]
        for d, cp in enumerate(ny):
            cp.wait_recv()
            total = total + ny_got[d]
        scale[0] = lax.rsqrt(total + F32(1e-6))
        pass_on.start()

    def product(u, parts, natural):
        for q in range(3):
            at = pl.ds(q * cols, cols)
            total = None
            for moved, still in parts:
                term = jnp.dot(moved[...], still[:, at], preferred_element_type=F32)
                total = term if total is None else total + term
            tbuf[:, at] = total
            nbuf[at, :] = total.T
        for g in range(NX):
            turned = nbuf[pl.ds(192 * g, 192), :].reshape(8, 3, 8, cols)
            for q in range(3):
                at = pl.ds(q * cols, cols)
                plain = tbuf[pl.ds(64 * g, 64), at]
                units[u, g, :, at] = jnp.where(natural, turned[:, q].reshape(64, cols), plain)

    def arrived(ref, sem):
        pltpu.make_async_copy(ref, ref, sem).wait()

    class Early:
        def __init__(self, k):
            self.k, self.sends = k, []
            self.base = 12 * k

        def group(self, g):
            return units.at[self.k, :, pl.ds(pl.multiple_of(8 * g, 8), 8)]

        def slot(self, step, side):
            return ry_half.at[self.k, side] if step == 0 else ry_full.at[self.k, step - 1, side]

        def out(self, step, srcs):
            for side in range(2):
                at = self.base + 2 * step + side
                cp = remote(
                    srcs[side], self.slot(step, side), sum_send.at[at], sum_recv.at[at], y=at_y(1 - 2 * side)
                )
                cp.start()
                self.sends.append(cp)

        def begin(self):
            far = self.group(at_y(NY // 2))
            self.out(0, [far.at[pl.ds(2 * side, 2)] for side in range(2)])

        def middle(self, step):
            last = self.sends[-2:]
            for side in range(2):
                last[side].wait_recv()
                where = self.group(at_y((NY // 2 - step) * (1 - 2 * side)))
                if step == 1:
                    where = where.at[pl.ds(2 * side, 2)]
                where[...] = where[...] + self.slot(step - 1, side)[...]
            self.out(step, [self.group(at_y((NY // 2 - step) * (1 - 2 * side))) for side in range(2)])

        def across(self):
            for cp in self.sends[-2:]:
                cp.wait_recv()
            deep = NY // 2 - 1
            wide[self.k, pl.ds(0, 4)] = self.group(y)[...] + self.slot(deep, 0)[...] + self.slot(deep, 1)[...]
            for d in range(1, NX):
                at = self.base + 7 + d
                cp = remote(
                    wide.at[self.k, at_x(d)], w_got.at[self.k, d], sum_send.at[at], sum_recv.at[at], x=at_x(d)
                )
                cp.start()
                self.sends.append(cp)

        def end(self):
            total = wide[self.k, x]
            for d in range(1, NX):
                self.sends[-NX + d].wait_recv()
                total = total + w_got[self.k, d]
            res[self.k] = total

    class Late:
        def __init__(self, k, away):
            self.k, self.u, self.away, self.sends = k, 3 + k, away, []
            self.base = 12 * self.u

        def begin(self):
            for d in (2, 1, 3):
                at = self.base + d
                cp = remote(
                    units.at[self.u, at_x(d)], rx_got.at[self.k, d - 1], sum_send.at[at], sum_recv.at[at], x=at_x(d)
                )
                cp.start()
                self.sends.append(cp)

        def across(self):
            total = units[self.u, x]
            for i, d in enumerate((2, 1, 3)):
                self.sends[i].wait_recv()
                total = total + rx_got[self.k, d - 1]
            wide[self.u] = total.reshape(8, 8, width)
            for d in (4, 3, 5, 2, 6, 1, 7, 0):
                at = self.base + 4 + d
                if self.away:
                    cp = remote(
                        wide.at[self.u, at_y(d)], w_got.at[self.k, d], sum_send.at[at], own_recv.at[8 * self.k + d],
                        z=z_up, c=0, y=at_y(d),
                    )
                elif d:
                    cp = remote(
                        wide.at[self.u, at_y(d)], w_got.at[self.u, d], sum_send.at[at], sum_recv.at[at], y=at_y(d)
                    )
                else:
                    continue
                cp.start()
                self.sends.append(cp)

        def end(self):
            total = wide[self.u, y]
            for i, d in enumerate((4, 3, 5, 2, 6, 1, 7)):
                self.sends[3 + i].wait_recv()
                total = total + w_got[self.u, d]
            res[self.u] = total

    def end_c(k):
        total = None
        for d in range(NY):
            arrived(w_got.at[k, d], own_recv.at[8 * k + d])
            total = w_got[k, d] if total is None else total + w_got[k, d]
        res[k] = total

    def finish_tile(direct, turned):
        total = None
        for k in range(3):
            out[0, pl.ds(8 * k, 8), :] = direct(k)
            piece = turned(k)
            piece = jnp.concatenate([piece[:, q * cols : (q + 1) * cols] for q in range(3)], axis=0)
            top = piece.astype(BF16).astype(F32)
            rest = piece - top
            mid = rest.astype(BF16).astype(F32)
            stack = jnp.concatenate([top, mid, rest - mid], axis=0).astype(BF16)
            term = jnp.dot(stack, shift[k], preferred_element_type=F32)
            total = term if total is None else total + term
        value = out[0] + (total[:24] + total[24:48] + total[48:])
        mine, other = scale[0], scale[1]
        left = jnp.where(own_first, mine, other)
        right = jnp.where(own_first, other, mine)
        i = lax.broadcasted_iota(jnp.int32, (24, width), 0)
        j = lax.broadcasted_iota(jnp.int32, (24, width), 1)
        down = jnp.sum(jnp.where(j == i + 24 * t, left, F32(0)), axis=1, keepdims=True)
        out[0] = value * down * right

    def wait_sends(*groups):
        for group in groups:
            for cp in group:
                cp.wait_send()

    nothing = jnp.zeros((8, width), F32)
    first_rows, last_rows = pl.ds(0, half), pl.ds(half, half)

    @pl.when(c == 0)
    def _():
        flags = remote(flag, flag_c, f_send, f_recv, z=z_down, c=1)
        to_c = [remote(sent.at[k, 1], got_c.at[k], z_send.at[k], z_recv.at[k], z=z_down, c=1) for k in range(3)]
        to_a = [
            [remote(sent.at[k, h], got.at[k, h], core_send.at[k, h], a_recv.at[k, h], c=1) for h in range(2)]
            for k in range(3)
        ]
        passed = remote(scale.at[0], scale.at[1], n_send.at[10], n_recv.at[10], c=1)
        for i in (2, 3):
            loads[i].wait()
        chunk(0, 1)
        pl.semaphore_wait(bar, NX + NY - 1 + NY)
        to_c[0].start()
        to_a[0][1].start()
        flags.start()
        for i in (0, 1):
            loads[i].wait()
        for k in range(3):
            if k:
                chunk(k, 1)
                to_c[k].start()
                to_a[k][1].start()
            chunk(k, 0)
            to_a[k][0].start()
        total = masks(0, half, [(nat, 0, jnp.maximum(onsets[own], onsets[low]))], nothing)
        norm_x(masks(half, rows, [], total))

        tiles = [Late(k, False) for k in range(3)]

        def make(k):
            arrived(got.at[k, 0], z_recv.at[k])
            product(3 + k, ((got.at[k, 0], nat.at[first_rows]),), own_first)
            tiles[k].begin()

        make(0)
        norm_y()
        make(1)
        tiles[0].across()
        norm_end(passed)
        make(2)
        tiles[1].across()
        tiles[0].end()
        end_c(0)
        tiles[2].across()
        tiles[1].end()
        end_c(1)
        tiles[2].end()
        end_c(2)
        arrived(scale.at[1], n_recv.at[10])
        finish_tile(
            lambda k: jnp.where(own_first, res[k], res[3 + k]), lambda k: jnp.where(own_first, res[3 + k], res[k])
        )
        wait_sends([flags, passed], to_c, nx, ny, *to_a, *(tile.sends for tile in tiles))

    @pl.when(c == 1)
    def _():
        to_b = [remote(sent.at[k, 0], got.at[k, 0], z_send.at[k], z_recv.at[k], z=z_up, c=0) for k in range(3)]
        passed = remote(scale.at[0], scale.at[1], n_send.at[10], n_recv.at[10], z=z_up, c=0)
        for i in (0, 1):
            loads[i].wait()
        chunk(0, 0)
        pl.semaphore_wait(bar, NX + NY - 1 + NY)
        to_b[0].start()
        for k in (1, 2):
            chunk(k, 0)
            to_b[k].start()
        for i in (2, 3):
            loads[i].wait()
        onset_a = jnp.maximum(onsets[own], onsets[low])
        onset_c = jnp.maximum(onsets[own], onsets[high])
        total = masks(0, half, [(nat, 0, onset_a)], nothing)
        norm_x(masks(half, rows, [(nat, 0, onset_a), (nat_c, half, onset_c)], total))

        early = [Early(k) for k in range(3)]
        late = [Late(k, True) for k in range(3)]

        def make_a(k):
            for h in range(2):
                arrived(got.at[k, h], a_recv.at[k, h])
            product(k, ((got.at[k, 0], nat.at[first_rows]), (got.at[k, 1], nat.at[last_rows])), own_first)
            early[k].begin()

        def make_c(k):
            if k == 0:
                arrived(flag_c, f_recv)
            arrived(got_c.at[k], z_recv.at[k])
            natural = jnp.broadcast_to(flag_c[0:1, 0:1] < F32(0.5), (64, cols))
            product(3 + k, ((got_c.at[k], nat_c),), natural)
            late[k].begin()

        for k in range(3):
            make_a(k)
        make_c(0)
        norm_y()
        for k in range(3):
            early[k].middle(1)
        make_c(1)
        late[0].across()
        norm_end(passed)
        for k in range(3):
            early[k].middle(2)
        make_c(2)
        late[1].across()
        for k in range(3):
            early[k].middle(3)
        late[2].across()
        for k in range(3):
            early[k].across()
        for k in range(3):
            early[k].end()
        arrived(scale.at[1], n_recv.at[10])
        finish_tile(
            lambda k: jnp.where(own_first, F32(0), res[k]), lambda k: jnp.where(own_first, res[k], F32(0))
        )
        wait_sends([passed], to_b, nx, ny, *(tile.sends for tile in early + late))


def on_device(greens, pairs, onsets):
    rows, width = greens.shape
    half, cols = rows // 2, width // 3
    vmem = pltpu.VMEM
    dma = pltpu.SemaphoreType.DMA
    return pl.pallas_call(
        kernel,
        out_shape=jax.ShapeDtypeStruct((1, width // (NX * NY), width), F32),
        in_specs=[
            pl.BlockSpec(memory_space=pl.ANY),
            pl.BlockSpec(memory_space=pltpu.SMEM),
            pl.BlockSpec(memory_space=pltpu.SMEM),
        ],
        out_specs=pl.BlockSpec(memory_space=vmem),
        scratch_shapes=[
            vmem((rows, width), BF16),
            vmem((rows, width), BF16),
            vmem((half, width), BF16),
            vmem((3, 2, cols, half), BF16),
            vmem((3, 2, cols, half), BF16),
            vmem((3, cols, half), BF16),
            vmem((3, cols, width), BF16),
            vmem((cols, width), F32),
            vmem((width, cols), F32),
            vmem((6, NX, 64, width), F32),
            vmem((3, NX - 1, 64, width), F32),
            vmem((3, 2, 2, 8, width), F32),
            vmem((3, 3, 2, 4, 8, width), F32),
            vmem((6, 8, 8, width), F32),
            vmem((6, 8, 8, width), F32),
            vmem((6, 8, width), F32),
            vmem((2, 1, width), F32),
            vmem((NX - 1, 1, width), F32),
            vmem((NY - 1, 1, width), F32),
            vmem((2, 1, width), F32),
            vmem((8, 128), F32),
            vmem((8, 128), F32),
            dma((4,)),
            dma((3,)),
            dma((3,)),
            dma((3, 2)),
            dma((3, 2)),
            dma((72,)),
            dma((72,)),
            dma((24,)),
            dma((11,)),
            dma((11,)),
            dma,
            dma,
        ],
        compiler_params=pltpu.CompilerParams(
            collective_id=0, has_side_effects=True, vmem_limit_bytes=56 * 1024 * 1024
        ),
        cost_estimate=pl.CostEstimate(flops=5_000_000_000, bytes_accessed=4_000_000, transcendentals=768),
    )(greens, pairs, onsets)


def solution(mesh):
    split = Mesh(mesh.devices.reshape(NZ, 2, NX, NY), ("z", "c", "x", "y"))
    in_specs = (P(("x", "y"), ("z", "c")), P(("z", "c"), None), P())
    out_specs = P(("z", "c"), ("x", "y"), None)
    return jax.shard_map(on_device, mesh=split, in_specs=in_specs, out_specs=out_specs, check_vma=False)
```

```python
import functools

import jax
import jax.numpy as jnp
from jax import lax
from jax.experimental import pallas as pl
from jax.experimental.pallas import tpu as pltpu
from jax.sharding import Mesh
from jax.sharding import PartitionSpec as P

MESH = pl.DeviceIdType.MESH
F32 = jnp.float32
BF16 = jnp.bfloat16
NZ, NX, NY = 8, 4, 8
FAR_FIRST = (4, 3, 5, 2, 6, 1, 7)


def remote(src, dst, send, recv, **where):
    return pltpu.make_async_remote_copy(
        src_ref=src, dst_ref=dst, send_sem=send, recv_sem=recv, device_id=where, device_id_type=MESH
    )


def kernel(
    greens, pairs, onsets, out,
    held, nat, nat_c, sent, got, got_c, shift, tbuf, nbuf, units, rx_got, ry_half, ry_full,
    wide, w_got, res, both, npart, nx_got, ny_got, scale, flag, flag_c,
    load_sem, z_send, z_recv, core_send, a_recv, sum_send, sum_recv, own_recv,
    n_send, n_recv, f_send, f_recv,
):
    z, c, x, y = (lax.axis_index(a) for a in ("z", "c", "x", "y"))
    rows, width = greens.shape
    half = rows // 2
    cols = width // 3
    t = x * NY + y
    row_start = t * rows
    z_up, z_down = lax.rem(z + 1, NZ), lax.rem(z + NZ - 1, NZ)
    own = 2 * z + c
    low = lax.rem(own + 2 * NZ - 1, 2 * NZ)
    high = lax.rem(own + 1, 2 * NZ)

    def at_x(d):
        return lax.rem(x + d + NX, NX)

    def at_y(d):
        return lax.rem(y + d + NY, NY)

    bar = pltpu.get_barrier_semaphore()

    def hello(**where):
        pl.semaphore_signal(bar, inc=1, device_id=where, device_id_type=MESH)

    loads = [
        pltpu.make_async_copy(
            greens.at[pl.ds(i * 512, 512)], held.at[pl.ds(i * 512, 512)], load_sem.at[i]
        )
        for i in range(rows // 512)
    ]
    for i in (2, 3, 0, 1):
        pl.when(c == 0)(loads[i].start)
    for i in (0, 1, 2, 3):
        pl.when(c == 1)(loads[i].start)
    hello(c=1 - c)

    @pl.when(c == 0)
    def _():
        hello(z=z_down, c=1)
        for d in range(NY):
            if d:
                hello(z=z_down, y=at_y(d), c=1)

    @pl.when(c == 1)
    def _():
        hello(z=z_up, c=0)
        for d in range(NY):
            if d:
                hello(z=z_up, y=at_y(d), c=0)

    for d in range(1, NX):
        hello(x=at_x(d))
    for d in range(1, NY):
        hello(y=at_y(d))

    for k in range(3):
        i = lax.broadcasted_iota(jnp.int32, (cols, width), 0)
        j = lax.broadcasted_iota(jnp.int32, (cols, width), 1)
        if k < 2:
            hit = j == i + 16 * lax.shift_right_logical(i, 3) + 8 * k
        else:
            h, rest = lax.shift_right_logical(i, 7), i & 127
            hit = j == rest + 20 * lax.shift_right_logical(rest, 2) + 16 + 4 * h
        shift[k] = jnp.where(hit, F32(1), F32(0)).astype(BF16)

    own_first = pairs[0, 0] == own
    flag[...] = jnp.where(own_first, jnp.ones_like(flag), jnp.zeros_like(flag))

    def chunk(k, h):
        for b in range(2):
            part = held[pl.ds(h * half + b * 512, 512), :]
            sent[k, h, :, pl.ds(b * 512, 512)] = lax.dot_general(
                shift[k], part, (((1,), (1,)), ((), ())), preferred_element_type=F32
            ).astype(BF16)

    def masks(first, last, targets, total):
        own_from = onsets[own] - row_start
        step = 64

        def body(i, total):
            at = pl.multiple_of(i * step, step)
            block = held[pl.ds(at, step), :].astype(F32)
            ids = at + lax.broadcasted_iota(jnp.int32, (step, width), 0)
            for ref, shifted, onset in targets:
                to = pl.multiple_of(at - shifted, step)
                ref[pl.ds(to, step), :] = jnp.where(ids >= onset - row_start, block, F32(0)).astype(BF16)
            mine = jnp.where(ids >= own_from, block, F32(0))
            return total + jnp.sum((mine * mine).reshape(step // 8, 8, width), axis=0)

        return lax.fori_loop(first // step, last // step, body, total)

    nx = [
        remote(npart.at[0], nx_got.at[d - 1], n_send.at[d - 1], n_recv.at[d - 1], x=at_x(d))
        for d in range(1, NX)
    ]
    ny = [
        remote(npart.at[1], ny_got.at[d - 1], n_send.at[2 + d], n_recv.at[2 + d], y=at_y(d))
        for d in range(1, NY)
    ]

    def norm_x(total):
        npart[0] = jnp.sum(total, axis=0, keepdims=True)
        for cp in nx:
            cp.start()

    def norm_y():
        total = npart[0]
        for d, cp in enumerate(nx):
            cp.wait_recv()
            total = total + nx_got[d]
        npart[1] = total
        for cp in ny:
            cp.start()

    def norm_end(pass_on):
        total = npart[1]
        for d, cp in enumerate(ny):
            cp.wait_recv()
            total = total + ny_got[d]
        scale[0] = lax.rsqrt(total + F32(1e-6))
        pass_on.start()

    def product(u, parts, natural):
        for q in range(3):
            at = pl.ds(q * cols, cols)
            total = None
            for moved, still in parts:
                term = jnp.dot(moved[...], still[:, at], preferred_element_type=F32)
                total = term if total is None else total + term
            tbuf[:, at] = total
            nbuf[at, :] = total.T
        for g in range(NX):
            turned = nbuf[pl.ds(192 * g, 192), :].reshape(8, 3, 8, cols)
            for q in range(3):
                at = pl.ds(q * cols, cols)
                plain = tbuf[pl.ds(64 * g, 64), at]
                units[u, g, :, at] = jnp.where(natural, turned[:, q].reshape(64, cols), plain)

    def product_half(u, h, parts, natural):
        total = None
        for moved, still in parts:
            term = jnp.dot(moved[...], still[...], preferred_element_type=F32)
            total = term if total is None else total + term
        half_cols, few = width // 2, cols // 2
        nbuf[:, pl.ds(0, few)] = total.T
        left, right = total[:, :half_cols], total[:, half_cols:]
        top = lax.broadcasted_iota(jnp.int32, (few, half_cols), 0) & 7 < 4
        even = jnp.where(top, left, pltpu.roll(right, 4, 0)).reshape(16, 1, 8, half_cols)
        odd = jnp.where(top, pltpu.roll(left, few - 4, 0), right).reshape(16, 1, 8, half_cols)
        tbuf[:, pl.ds(0, half_cols)] = jnp.concatenate([even, odd], axis=1).reshape(cols, half_cols)
        for g in range(NX):
            turned = nbuf[pl.ds(192 * g, 192), pl.ds(0, few)].reshape(8, 3, 8, few)
            for q in range(3):
                plain = tbuf[pl.ds(64 * g, 64), pl.ds(q * few, few)]
                to = pl.ds(h * half_cols + q * few, few)
                units[u, g, :, to] = jnp.where(natural[:, :few], turned[:, q].reshape(64, few), plain)

    def arrived(ref, sem):
        pltpu.make_async_copy(ref, ref, sem).wait()

    class Chunk:
        def __init__(self, u, slot, first=0, count=None, away=None):
            self.u, self.away, self.sends, self.base = u, away, [], 12 * slot
            self.cut = pl.ds(first, width if count is None else count)

        def go(self, index, src, dst, sem=None, **where):
            at = self.base + index
            cp = remote(src, dst, sum_send.at[at], sum_recv.at[at] if sem is None else sem, **where)
            cp.start()
            self.sends.append(cp)

        def y_rows(self, g):
            return units.at[self.u, :, pl.ds(pl.multiple_of(8 * g, 8), 8), self.cut]

        def x_ends(self):
            for d in range(1, NX):
                self.go(7 + d, wide.at[self.u, at_x(d), :, self.cut], w_got.at[self.u, d, :, self.cut], x=at_x(d))

        def end(self):
            total = wide[self.u, x, :, self.cut]
            for d in range(1, NX):
                self.sends[-NX + d].wait_recv()
                total = total + w_got[self.u, d, :, self.cut]
            res[self.u, :, self.cut] = total

    class RingY(Chunk):
        def slot(self, step, side):
            return ry_half.at[self.u, side] if step == 0 else ry_full.at[self.u, step - 1, side]

        def both(self, step, srcs):
            for side in range(2):
                self.go(2 * step + side, srcs[side], self.slot(step, side), y=at_y(1 - 2 * side))

        def begin(self):
            far = self.y_rows(at_y(NY // 2))
            self.both(0, [far.at[pl.ds(2 * side, 2)] for side in range(2)])

        def middle(self, step):
            last = self.sends[-2:]
            for side in range(2):
                last[side].wait_recv()
                where = self.y_rows(at_y((NY // 2 - step) * (1 - 2 * side)))
                if step == 1:
                    where = where.at[pl.ds(2 * side, 2)]
                where[...] = where[...] + self.slot(step - 1, side)[...]
            self.both(step, [self.y_rows(at_y((NY // 2 - step) * (1 - 2 * side))) for side in range(2)])

        def across(self):
            for cp in self.sends[-2:]:
                cp.wait_recv()
            deep = NY // 2 - 1
            wide[self.u, pl.ds(0, 4)] = self.y_rows(y)[...] + self.slot(deep, 0)[...] + self.slot(deep, 1)[...]
            self.x_ends()

    class AllX(Chunk):
        def begin(self):
            for d in (2, 1, 3):
                self.go(
                    d, units.at[self.u, at_x(d), :, self.cut], rx_got.at[self.u, d - 1, :, self.cut], x=at_x(d)
                )

        def across(self):
            total = units[self.u, x, :, self.cut]
            for i, d in enumerate((2, 1, 3)):
                self.sends[i].wait_recv()
                total = total + rx_got[self.u, d - 1, :, self.cut]
            wide[self.u, :, :, self.cut] = total.reshape(8, 8, -1)
            for d in FAR_FIRST + ((0,) if self.away is not None else ()):
                src, dst = wide.at[self.u, at_y(d), :, self.cut], w_got.at[self.u, d, :, self.cut]
                if self.away is None:
                    self.go(4 + d, src, dst, y=at_y(d))
                else:
                    self.go(4 + d, src, dst, own_recv.at[8 * self.away + d], z=z_up, c=0, y=at_y(d))

        def end(self):
            total = wide[self.u, y, :, self.cut]
            for i, d in enumerate(FAR_FIRST):
                self.sends[3 + i].wait_recv()
                total = total + w_got[self.u, d, :, self.cut]
            res[self.u, :, self.cut] = total

    def end_c(k, away, first=0, count=None):
        total = None
        cut = pl.ds(first, width if count is None else count)
        for d in range(NY):
            arrived(w_got.at[3 + k, d, :, cut], own_recv.at[8 * away + d])
            total = w_got[3 + k, d, :, cut] if total is None else total + w_got[3 + k, d, :, cut]
        res[3 + k, :, cut] = total

    def put_back(piece, k):
        top = piece.astype(BF16).astype(F32)
        rest = piece - top
        mid = rest.astype(BF16).astype(F32)
        stack = jnp.concatenate([top, mid, rest - mid], axis=0).astype(BF16)
        total = jnp.dot(stack, shift[k], preferred_element_type=F32)
        return total[:24] + total[24:48] + total[48:]

    def finish_early(direct, turned):
        total = None
        for k in range(2):
            piece = turned(k)
            piece = jnp.concatenate([piece[:, q * cols : (q + 1) * cols] for q in range(3)], axis=0)
            term = put_back(piece, k)
            total = term if total is None else total + term
        out[0] = total
        for k in range(2):
            out[0, pl.ds(8 * k, 8), :] = out[0, pl.ds(8 * k, 8), :] + direct(k)
        mine, other = scale[0], scale[1]
        left = jnp.where(own_first, mine, other)
        right = jnp.where(own_first, other, mine)
        i = lax.broadcasted_iota(jnp.int32, (24, width), 0)
        j = lax.broadcasted_iota(jnp.int32, (24, width), 1)
        down = jnp.sum(jnp.where(j == i + 24 * t, left, F32(0)), axis=1, keepdims=True)
        both[...] = down * right

    def finish(direct, turned):
        few, half_cols = cols // 2, width // 2
        piece = turned(2)
        piece = jnp.concatenate(
            [
                jnp.concatenate([piece[:, h * half_cols + q * few : h * half_cols + (q + 1) * few] for q in range(3)], axis=0)
                for h in range(2)
            ],
            axis=1,
        )
        value = out[0] + put_back(piece, 2)
        straight = direct(2)
        low_half, high_half = straight[:, :half_cols], straight[:, half_cols:]
        top = lax.broadcasted_iota(jnp.int32, (8, half_cols), 0) < 4
        straight = jnp.concatenate(
            [
                jnp.where(top, low_half, pltpu.roll(high_half, 4, 0)),
                jnp.where(top, pltpu.roll(low_half, 4, 0), high_half),
            ],
            axis=1,
        )
        out[0, pl.ds(0, 16), :] = value[:16] * both[pl.ds(0, 16), :]
        out[0, pl.ds(16, 8), :] = (value[16:] + straight) * both[pl.ds(16, 8), :]

    def wait_sends(*groups):
        for group in groups:
            for cp in group:
                cp.wait_send()

    whole, halves = pl.ds(0, cols), [pl.ds(cols // 2 * h, cols // 2) for h in range(2)]
    pieces = [(0, whole), (1, whole), (2, halves[0]), (2, halves[1])]
    half_width = width // 2
    nothing = jnp.zeros((8, width), F32)
    first_rows, last_rows = pl.ds(0, half), pl.ds(half, half)

    @pl.when(c == 0)
    def _():
        flags = remote(flag, flag_c, f_send, f_recv, z=z_down, c=1)
        to_c = [
            remote(sent.at[k, 1, r], got_c.at[k, r], z_send.at[i], z_recv.at[i], z=z_down, c=1)
            for i, (k, r) in enumerate(pieces)
        ]
        to_a = [
            [remote(sent.at[k, h], got.at[k, h], core_send.at[k, h], a_recv.at[k, h], c=1) for h in range(2)]
            for k in range(3)
        ]
        passed = remote(scale.at[0], scale.at[1], n_send.at[10], n_recv.at[10], c=1)
        for i in (2, 3):
            loads[i].wait()
        chunk(0, 1)
        pl.semaphore_wait(bar, NX + NY - 1 + NY)
        to_c[0].start()
        to_a[0][1].start()
        flags.start()
        for i in (0, 1):
            loads[i].wait()
        for k in range(3):
            if k:
                chunk(k, 1)
                to_c[k].start()
                if k == 2:
                    to_c[3].start()
                to_a[k][1].start()
            chunk(k, 0)
            to_a[k][0].start()
        total = masks(0, half, [(nat, 0, jnp.maximum(onsets[own], onsets[low]))], nothing)
        norm_x(masks(half, rows, [], total))

        tiles = [RingY(0, 0), RingY(1, 1)]
        last = [AllX(2, 2, 0, half_width), AllX(2, 6, half_width, half_width)]

        def make(k):
            arrived(got.at[k, 0], z_recv.at[k])
            product(k, ((got.at[k, 0], nat.at[first_rows]),), own_first)
            tiles[k].begin()

        def make_last(h):
            moved = got.at[2, 0, halves[h]]
            arrived(moved, z_recv.at[2 + h])
            product_half(2, h, ((moved, nat.at[first_rows]),), jnp.broadcast_to(own_first, (64, cols)))
            last[h].begin()

        make(0)
        norm_y()
        tiles[0].middle(1)
        make(1)
        tiles[0].middle(2)
        norm_end(passed)
        tiles[1].middle(1)
        make_last(0)
        make_last(1)
        tiles[0].middle(3)
        tiles[1].middle(2)
        last[0].across()
        tiles[0].across()
        tiles[1].middle(3)
        last[1].across()
        tiles[0].end()
        end_c(0, 0)
        tiles[1].across()
        wait_sends([flags, passed], to_c, nx, ny, *to_a, tiles[0].sends)
        arrived(scale.at[1], n_recv.at[10])
        end_c(1, 1)
        tiles[1].end()
        direct = lambda k: jnp.where(own_first, res[3 + k], res[k])
        turned = lambda k: jnp.where(own_first, res[k], res[3 + k])
        finish_early(direct, turned)
        wait_sends(tiles[1].sends)
        for h in range(2):
            last[h].end()
            end_c(2, 2 + h, half_width * h, half_width)
        finish(direct, turned)
        wait_sends(last[0].sends, last[1].sends)

    @pl.when(c == 1)
    def _():
        to_b = [
            remote(sent.at[k, 0, r], got.at[k, 0, r], z_send.at[i], z_recv.at[i], z=z_up, c=0)
            for i, (k, r) in enumerate(pieces)
        ]
        passed = remote(scale.at[0], scale.at[1], n_send.at[10], n_recv.at[10], z=z_up, c=0)
        for i in (0, 1):
            loads[i].wait()
        chunk(0, 0)
        pl.semaphore_wait(bar, NX + NY - 1 + NY)
        to_b[0].start()
        for k in (1, 2):
            chunk(k, 0)
            to_b[k].start()
        to_b[3].start()
        for i in (2, 3):
            loads[i].wait()
        onset_a = jnp.maximum(onsets[own], onsets[low])
        onset_c = jnp.maximum(onsets[own], onsets[high])
        total = masks(0, half, [(nat, 0, onset_a)], nothing)
        norm_x(masks(half, rows, [(nat, 0, onset_a), (nat_c, half, onset_c)], total))

        early = [AllX(0, 0), RingY(1, 1), RingY(2, 2)]
        late = [AllX(3, 3, away=0), AllX(4, 4, away=1)]
        last = [AllX(5, 5, 0, half_width, 2), AllX(5, 7, half_width, half_width, 3)]

        def make_a(k):
            for h in range(2):
                arrived(got.at[k, h], a_recv.at[k, h])
            if k < 2:
                product(k, ((got.at[k, 0], nat.at[first_rows]), (got.at[k, 1], nat.at[last_rows])), own_first)
            else:
                for h in range(2):
                    parts = ((got.at[2, 0, halves[h]], nat.at[first_rows]), (got.at[2, 1, halves[h]], nat.at[last_rows]))
                    product_half(2, h, parts, jnp.broadcast_to(own_first, (64, cols)))
            early[k].begin()

        def natural_c():
            return jnp.broadcast_to(flag_c[0:1, 0:1] < F32(0.5), (64, cols))

        def make_c(k):
            if k == 0:
                arrived(flag_c, f_recv)
            arrived(got_c.at[k], z_recv.at[k])
            product(3 + k, ((got_c.at[k], nat_c),), natural_c())
            late[k].begin()

        def make_last(h):
            moved = got_c.at[2, halves[h]]
            arrived(moved, z_recv.at[2 + h])
            product_half(5, h, ((moved, nat_c),), natural_c())
            last[h].begin()

        make_a(0)
        make_a(1)
        make_c(0)
        make_a(2)
        norm_y()
        early[0].across()
        for k in range(1, 3):
            early[k].middle(1)
        make_c(1)
        late[0].across()
        norm_end(passed)
        for k in range(1, 3):
            early[k].middle(2)
        make_last(0)
        for k in range(1, 3):
            early[k].middle(3)
        late[1].across()
        make_last(1)
        last[0].across()
        for k in range(1, 3):
            early[k].across()
        last[1].across()
        wait_sends([passed], to_b, nx, ny, late[0].sends, late[1].sends)
        arrived(scale.at[1], n_recv.at[10])
        early[0].end()
        early[1].end()
        direct = lambda k: jnp.where(own_first, F32(0), res[k])
        turned = lambda k: jnp.where(own_first, res[k], F32(0))
        finish_early(direct, turned)
        early[2].end()
        finish(direct, turned)
        wait_sends(*(tile.sends for tile in early + last))


def on_device(greens, pairs, onsets):
    rows, width = greens.shape
    half, cols = rows // 2, width // 3
    vmem = pltpu.VMEM
    dma = pltpu.SemaphoreType.DMA
    return pl.pallas_call(
        kernel,
        out_shape=jax.ShapeDtypeStruct((1, width // (NX * NY), width), F32),
        in_specs=[
            pl.BlockSpec(memory_space=pl.ANY),
            pl.BlockSpec(memory_space=pltpu.SMEM),
            pl.BlockSpec(memory_space=pltpu.SMEM),
        ],
        out_specs=pl.BlockSpec(memory_space=vmem),
        scratch_shapes=[
            vmem((rows, width), BF16),
            vmem((rows, width), BF16),
            vmem((half, width), BF16),
            vmem((3, 2, cols, half), BF16),
            vmem((3, 2, cols, half), BF16),
            vmem((3, cols, half), BF16),
            vmem((3, cols, width), BF16),
            vmem((cols, width), F32),
            vmem((width, cols), F32),
            vmem((6, NX, 64, width), F32),
            vmem((6, NX - 1, 64, width), F32),
            vmem((3, 2, 2, 8, width), F32),
            vmem((3, 3, 2, 4, 8, width), F32),
            vmem((6, 8, 8, width), F32),
            vmem((6, 8, 8, width), F32),
            vmem((6, 8, width), F32),
            vmem((24, width), F32),
            vmem((2, 1, width), F32),
            vmem((NX - 1, 1, width), F32),
            vmem((NY - 1, 1, width), F32),
            vmem((2, 1, width), F32),
            vmem((8, 128), F32),
            vmem((8, 128), F32),
            dma((4,)),
            dma((4,)),
            dma((4,)),
            dma((3, 2)),
            dma((3, 2)),
            dma((96,)),
            dma((96,)),
            dma((32,)),
            dma((11,)),
            dma((11,)),
            dma,
            dma,
        ],
        compiler_params=pltpu.CompilerParams(
            collective_id=0, has_side_effects=True, vmem_limit_bytes=56 * 1024 * 1024
        ),
        cost_estimate=pl.CostEstimate(flops=5_000_000_000, bytes_accessed=4_000_000, transcendentals=768),
    )(greens, pairs, onsets)


def solution(mesh):
    split = Mesh(mesh.devices.reshape(NZ, 2, NX, NY), ("z", "c", "x", "y"))
    in_specs = (P(("x", "y"), ("z", "c")), P(("z", "c"), None), P())
    out_specs = P(("z", "c"), ("x", "y"), None)
    return jax.shard_map(on_device, mesh=split, in_specs=in_specs, out_specs=out_specs, check_vma=False)
```

```python
import functools

import jax
import jax.numpy as jnp
from jax import lax
from jax.experimental import pallas as pl
from jax.experimental.pallas import tpu as pltpu
from jax.sharding import Mesh
from jax.sharding import PartitionSpec as P

MESH = pl.DeviceIdType.MESH
F32 = jnp.float32
BF16 = jnp.bfloat16
NZ, NX, NY = 8, 4, 8
FAR_FIRST = (4, 3, 5, 2, 6, 1, 7)


def remote(src, dst, send, recv, **where):
    return pltpu.make_async_remote_copy(
        src_ref=src, dst_ref=dst, send_sem=send, recv_sem=recv, device_id=where, device_id_type=MESH
    )


def kernel(
    greens, pairs, onsets, out,
    held, nat, nat_c, sent, got, got_c, shift, tbuf, nbuf, units, rx_got, ry_half, ry_full,
    wide, w_got, res, both, npart, nx_got, ny_got, scale, flag, flag_c,
    load_sem, z_send, z_recv, core_send, a_recv, sum_send, sum_recv, own_recv,
    n_send, n_recv, f_send, f_recv,
):
    z, c, x, y = (lax.axis_index(a) for a in ("z", "c", "x", "y"))
    rows, width = greens.shape
    half = rows // 2
    cols = width // 3
    t = x * NY + y
    row_start = t * rows
    z_up, z_down = lax.rem(z + 1, NZ), lax.rem(z + NZ - 1, NZ)
    own = 2 * z + c
    low = lax.rem(own + 2 * NZ - 1, 2 * NZ)
    high = lax.rem(own + 1, 2 * NZ)

    def at_x(d):
        return lax.rem(x + d + NX, NX)

    def at_y(d):
        return lax.rem(y + d + NY, NY)

    bar = pltpu.get_barrier_semaphore()

    def hello(**where):
        pl.semaphore_signal(bar, inc=1, device_id=where, device_id_type=MESH)

    loads = [
        pltpu.make_async_copy(
            greens.at[pl.ds(i * 512, 512)], held.at[pl.ds(i * 512, 512)], load_sem.at[i]
        )
        for i in range(rows // 512)
    ]
    for i in (2, 3, 0, 1):
        pl.when(c == 0)(loads[i].start)
    for i in (0, 1, 2, 3):
        pl.when(c == 1)(loads[i].start)
    hello(c=1 - c)

    @pl.when(c == 0)
    def _():
        hello(z=z_down, c=1)
        for d in range(NY):
            if d:
                hello(z=z_down, y=at_y(d), c=1)

    @pl.when(c == 1)
    def _():
        hello(z=z_up, c=0)
        for d in range(NY):
            if d:
                hello(z=z_up, y=at_y(d), c=0)

    for d in range(1, NX):
        hello(x=at_x(d))
    for d in range(1, NY):
        hello(y=at_y(d))

    for k in range(3):
        i = lax.broadcasted_iota(jnp.int32, (cols, width), 0)
        j = lax.broadcasted_iota(jnp.int32, (cols, width), 1)
        if k < 2:
            hit = j == i + 16 * lax.shift_right_logical(i, 3) + 8 * k
        else:
            h, rest = lax.shift_right_logical(i, 7), i & 127
            hit = j == rest + 20 * lax.shift_right_logical(rest, 2) + 16 + 4 * h
        shift[k] = jnp.where(hit, F32(1), F32(0)).astype(BF16)

    own_first = pairs[0, 0] == own
    flag[...] = jnp.where(own_first, jnp.ones_like(flag), jnp.zeros_like(flag))

    def chunk(k, h):
        for b in range(2):
            part = held[pl.ds(h * half + b * 512, 512), :]
            sent[k, h, :, pl.ds(b * 512, 512)] = lax.dot_general(
                shift[k], part, (((1,), (1,)), ((), ())), preferred_element_type=F32
            ).astype(BF16)

    def masks(first, last, targets, total):
        own_from = onsets[own] - row_start
        step = 64

        def body(i, total):
            at = pl.multiple_of(i * step, step)
            block = held[pl.ds(at, step), :].astype(F32)
            ids = at + lax.broadcasted_iota(jnp.int32, (step, width), 0)
            for ref, shifted, onset in targets:
                to = pl.multiple_of(at - shifted, step)
                ref[pl.ds(to, step), :] = jnp.where(ids >= onset - row_start, block, F32(0)).astype(BF16)
            mine = jnp.where(ids >= own_from, block, F32(0))
            return total + jnp.sum((mine * mine).reshape(step // 8, 8, width), axis=0)

        return lax.fori_loop(first // step, last // step, body, total)

    nx = [
        remote(npart.at[0], nx_got.at[d - 1], n_send.at[d - 1], n_recv.at[d - 1], x=at_x(d))
        for d in range(1, NX)
    ]
    ny = [
        remote(npart.at[1], ny_got.at[d - 1], n_send.at[2 + d], n_recv.at[2 + d], y=at_y(d))
        for d in range(1, NY)
    ]

    def norm_x(total):
        npart[0] = jnp.sum(total, axis=0, keepdims=True)
        for cp in nx:
            cp.start()

    def norm_y():
        total = npart[0]
        for d, cp in enumerate(nx):
            cp.wait_recv()
            total = total + nx_got[d]
        npart[1] = total
        for cp in ny:
            cp.start()

    def norm_end(pass_on):
        total = npart[1]
        for d, cp in enumerate(ny):
            cp.wait_recv()
            total = total + ny_got[d]
        scale[0] = lax.rsqrt(total + F32(1e-6))
        pass_on.start()

    def product(u, parts, natural):
        for q in range(3):
            at = pl.ds(q * cols, cols)
            total = None
            for moved, still in parts:
                term = jnp.dot(moved[...], still[:, at], preferred_element_type=F32)
                total = term if total is None else total + term
            tbuf[:, at] = total
            nbuf[at, :] = total.T
        for g in range(NX):
            turned = nbuf[pl.ds(192 * g, 192), :].reshape(8, 3, 8, cols)
            for q in range(3):
                at = pl.ds(q * cols, cols)
                plain = tbuf[pl.ds(64 * g, 64), at]
                units[u, g, :, at] = jnp.where(natural, turned[:, q].reshape(64, cols), plain)

    def product_half(u, h, parts, natural):
        total = None
        for moved, still in parts:
            term = jnp.dot(moved[...], still[...], preferred_element_type=F32)
            total = term if total is None else total + term
        half_cols, few = width // 2, cols // 2
        nbuf[:, pl.ds(0, few)] = total.T
        left, right = total[:, :half_cols], total[:, half_cols:]
        top = lax.broadcasted_iota(jnp.int32, (few, half_cols), 0) & 7 < 4
        even = jnp.where(top, left, pltpu.roll(right, 4, 0)).reshape(16, 1, 8, half_cols)
        odd = jnp.where(top, pltpu.roll(left, few - 4, 0), right).reshape(16, 1, 8, half_cols)
        tbuf[:, pl.ds(0, half_cols)] = jnp.concatenate([even, odd], axis=1).reshape(cols, half_cols)
        for g in range(NX):
            turned = nbuf[pl.ds(192 * g, 192), pl.ds(0, few)].reshape(8, 3, 8, few)
            for q in range(3):
                plain = tbuf[pl.ds(64 * g, 64), pl.ds(q * few, few)]
                to = pl.ds(h * half_cols + q * few, few)
                units[u, g, :, to] = jnp.where(natural[:, :few], turned[:, q].reshape(64, few), plain)

    def arrived(ref, sem):
        pltpu.make_async_copy(ref, ref, sem).wait()

    class Chunk:
        def __init__(self, u, slot, first=0, count=None, away=None):
            self.u, self.away, self.sends, self.base = u, away, [], 12 * slot
            self.cut = pl.ds(first, width if count is None else count)

        def go(self, index, src, dst, sem=None, **where):
            at = self.base + index
            cp = remote(src, dst, sum_send.at[at], sum_recv.at[at] if sem is None else sem, **where)
            cp.start()
            self.sends.append(cp)

        def y_rows(self, g):
            return units.at[self.u, :, pl.ds(pl.multiple_of(8 * g, 8), 8), self.cut]

        def x_ends(self):
            for d in range(1, NX):
                self.go(7 + d, wide.at[self.u, at_x(d), :, self.cut], w_got.at[self.u, d, :, self.cut], x=at_x(d))

        def end(self):
            total = wide[self.u, x, :, self.cut]
            for d in range(1, NX):
                self.sends[-NX + d].wait_recv()
                total = total + w_got[self.u, d, :, self.cut]
            res[self.u, :, self.cut] = total

    class RingY(Chunk):
        def slot(self, step, side):
            return ry_half.at[self.u, side] if step == 0 else ry_full.at[self.u, step - 1, side]

        def both(self, step, srcs):
            for side in range(2):
                self.go(2 * step + side, srcs[side], self.slot(step, side), y=at_y(1 - 2 * side))

        def begin(self):
            far = self.y_rows(at_y(NY // 2))
            self.both(0, [far.at[pl.ds(2 * side, 2)] for side in range(2)])

        def middle(self, step):
            last = self.sends[-2:]
            for side in range(2):
                last[side].wait_recv()
                where = self.y_rows(at_y((NY // 2 - step) * (1 - 2 * side)))
                if step == 1:
                    where = where.at[pl.ds(2 * side, 2)]
                where[...] = where[...] + self.slot(step - 1, side)[...]
            self.both(step, [self.y_rows(at_y((NY // 2 - step) * (1 - 2 * side))) for side in range(2)])

        def across(self):
            for cp in self.sends[-2:]:
                cp.wait_recv()
            deep = NY // 2 - 1
            wide[self.u, pl.ds(0, 4)] = self.y_rows(y)[...] + self.slot(deep, 0)[...] + self.slot(deep, 1)[...]
            self.x_ends()

    class AllX(Chunk):
        def begin(self):
            for d in (2, 1, 3):
                self.go(
                    d, units.at[self.u, at_x(d), :, self.cut], rx_got.at[self.u, d - 1, :, self.cut], x=at_x(d)
                )

        def across(self):
            total = units[self.u, x, :, self.cut]
            for i, d in enumerate((2, 1, 3)):
                self.sends[i].wait_recv()
                total = total + rx_got[self.u, d - 1, :, self.cut]
            wide[self.u, :, :, self.cut] = total.reshape(8, 8, -1)
            for d in FAR_FIRST + ((0,) if self.away is not None else ()):
                src, dst = wide.at[self.u, at_y(d), :, self.cut], w_got.at[self.u, d, :, self.cut]
                if self.away is None:
                    self.go(4 + d, src, dst, y=at_y(d))
                else:
                    self.go(4 + d, src, dst, own_recv.at[8 * self.away + d], z=z_up, c=0, y=at_y(d))

        def end(self):
            total = wide[self.u, y, :, self.cut]
            for i, d in enumerate(FAR_FIRST):
                self.sends[3 + i].wait_recv()
                total = total + w_got[self.u, d, :, self.cut]
            res[self.u, :, self.cut] = total

    def end_c(k, away, first=0, count=None):
        total = None
        cut = pl.ds(first, width if count is None else count)
        for d in range(NY):
            arrived(w_got.at[3 + k, d, :, cut], own_recv.at[8 * away + d])
            total = w_got[3 + k, d, :, cut] if total is None else total + w_got[3 + k, d, :, cut]
        res[3 + k, :, cut] = total

    def put_back(piece, k):
        top = piece.astype(BF16).astype(F32)
        rest = piece - top
        mid = rest.astype(BF16).astype(F32)
        stack = jnp.concatenate([top, mid, rest - mid], axis=0).astype(BF16)
        total = jnp.dot(stack, shift[k], preferred_element_type=F32)
        return total[:24] + total[24:48] + total[48:]

    def finish_early(direct, turned):
        total = None
        for k in range(2):
            piece = turned(k)
            piece = jnp.concatenate([piece[:, q * cols : (q + 1) * cols] for q in range(3)], axis=0)
            term = put_back(piece, k)
            total = term if total is None else total + term
        out[0] = total
        for k in range(2):
            out[0, pl.ds(8 * k, 8), :] = out[0, pl.ds(8 * k, 8), :] + direct(k)
        mine, other = scale[0], scale[1]
        left = jnp.where(own_first, mine, other)
        right = jnp.where(own_first, other, mine)
        i = lax.broadcasted_iota(jnp.int32, (24, width), 0)
        j = lax.broadcasted_iota(jnp.int32, (24, width), 1)
        down = jnp.sum(jnp.where(j == i + 24 * t, left, F32(0)), axis=1, keepdims=True)
        both[...] = down * right

    def finish(direct, turned):
        few, half_cols = cols // 2, width // 2
        piece = turned(2)
        piece = jnp.concatenate(
            [
                jnp.concatenate([piece[:, h * half_cols + q * few : h * half_cols + (q + 1) * few] for q in range(3)], axis=0)
                for h in range(2)
            ],
            axis=1,
        )
        value = out[0] + put_back(piece, 2)
        straight = direct(2)
        low_half, high_half = straight[:, :half_cols], straight[:, half_cols:]
        top = lax.broadcasted_iota(jnp.int32, (8, half_cols), 0) < 4
        straight = jnp.concatenate(
            [
                jnp.where(top, low_half, pltpu.roll(high_half, 4, 0)),
                jnp.where(top, pltpu.roll(low_half, 4, 0), high_half),
            ],
            axis=1,
        )
        out[0, pl.ds(0, 16), :] = value[:16] * both[pl.ds(0, 16), :]
        out[0, pl.ds(16, 8), :] = (value[16:] + straight) * both[pl.ds(16, 8), :]

    def wait_sends(*groups):
        for group in groups:
            for cp in group:
                cp.wait_send()

    whole, halves = pl.ds(0, cols), [pl.ds(cols // 2 * h, cols // 2) for h in range(2)]
    pieces = [(0, whole), (1, whole), (2, halves[0]), (2, halves[1])]
    half_width = width // 2
    nothing = jnp.zeros((8, width), F32)
    first_rows, last_rows = pl.ds(0, half), pl.ds(half, half)

    @pl.when(c == 0)
    def _():
        flags = remote(flag, flag_c, f_send, f_recv, z=z_down, c=1)
        to_c = [
            remote(sent.at[k, 1, r], got_c.at[k, r], z_send.at[i], z_recv.at[i], z=z_down, c=1)
            for i, (k, r) in enumerate(pieces)
        ]
        to_a = [
            [remote(sent.at[k, h], got.at[k, h], core_send.at[k, h], a_recv.at[k, h], c=1) for h in range(2)]
            for k in range(3)
        ]
        passed = remote(scale.at[0], scale.at[1], n_send.at[10], n_recv.at[10], c=1)
        for i in (2, 3):
            loads[i].wait()
        chunk(0, 1)
        pl.semaphore_wait(bar, NX + NY - 1 + NY)
        to_c[0].start()
        to_a[0][1].start()
        flags.start()
        for i in (0, 1):
            loads[i].wait()
        for k in range(3):
            if k:
                chunk(k, 1)
                to_c[k].start()
                if k == 2:
                    to_c[3].start()
                to_a[k][1].start()
            chunk(k, 0)
            to_a[k][0].start()
        total = masks(0, half, [(nat, 0, jnp.maximum(onsets[own], onsets[low]))], nothing)
        norm_x(masks(half, rows, [], total))

        tiles = [RingY(0, 0), RingY(1, 1)]
        last = [AllX(2, 2, 0, half_width), AllX(2, 6, half_width, half_width)]

        def make(k):
            arrived(got.at[k, 0], z_recv.at[k])
            product(k, ((got.at[k, 0], nat.at[first_rows]),), own_first)
            tiles[k].begin()

        def make_last(h):
            moved = got.at[2, 0, halves[h]]
            arrived(moved, z_recv.at[2 + h])
            product_half(2, h, ((moved, nat.at[first_rows]),), jnp.broadcast_to(own_first, (64, cols)))
            last[h].begin()

        make(0)
        norm_y()
        tiles[0].middle(1)
        make(1)
        tiles[0].middle(2)
        make_last(0)
        tiles[1].middle(1)
        make_last(1)
        norm_end(passed)
        tiles[0].middle(3)
        tiles[1].middle(2)
        last[0].across()
        tiles[0].across()
        tiles[1].middle(3)
        last[1].across()
        tiles[0].end()
        end_c(0, 0)
        tiles[1].across()
        wait_sends([flags, passed], to_c, nx, ny, *to_a, tiles[0].sends)
        arrived(scale.at[1], n_recv.at[10])
        end_c(1, 1)
        tiles[1].end()
        direct = lambda k: jnp.where(own_first, res[3 + k], res[k])
        turned = lambda k: jnp.where(own_first, res[k], res[3 + k])
        finish_early(direct, turned)
        wait_sends(tiles[1].sends)
        for h in range(2):
            last[h].end()
            end_c(2, 2 + h, half_width * h, half_width)
        finish(direct, turned)
        wait_sends(last[0].sends, last[1].sends)

    @pl.when(c == 1)
    def _():
        to_b = [
            remote(sent.at[k, 0, r], got.at[k, 0, r], z_send.at[i], z_recv.at[i], z=z_up, c=0)
            for i, (k, r) in enumerate(pieces)
        ]
        passed = remote(scale.at[0], scale.at[1], n_send.at[10], n_recv.at[10], z=z_up, c=0)
        for i in (0, 1):
            loads[i].wait()
        chunk(0, 0)
        pl.semaphore_wait(bar, NX + NY - 1 + NY)
        to_b[0].start()
        for k in (1, 2):
            chunk(k, 0)
            to_b[k].start()
        to_b[3].start()
        for i in (2, 3):
            loads[i].wait()
        onset_a = jnp.maximum(onsets[own], onsets[low])
        onset_c = jnp.maximum(onsets[own], onsets[high])
        total = masks(0, half, [(nat, 0, onset_a)], nothing)
        norm_x(masks(half, rows, [(nat, 0, onset_a), (nat_c, half, onset_c)], total))

        early = [AllX(0, 0), RingY(1, 1), RingY(2, 2)]
        late = [AllX(3, 3, away=0), AllX(4, 4, away=1)]
        last = [AllX(5, 5, 0, half_width, 2), AllX(5, 7, half_width, half_width, 3)]

        def make_a(k):
            for h in range(2):
                arrived(got.at[k, h], a_recv.at[k, h])
            if k < 2:
                product(k, ((got.at[k, 0], nat.at[first_rows]), (got.at[k, 1], nat.at[last_rows])), own_first)
            else:
                for h in range(2):
                    parts = ((got.at[2, 0, halves[h]], nat.at[first_rows]), (got.at[2, 1, halves[h]], nat.at[last_rows]))
                    product_half(2, h, parts, jnp.broadcast_to(own_first, (64, cols)))
            early[k].begin()

        def natural_c():
            return jnp.broadcast_to(flag_c[0:1, 0:1] < F32(0.5), (64, cols))

        def make_c(k):
            if k == 0:
                arrived(flag_c, f_recv)
            arrived(got_c.at[k], z_recv.at[k])
            product(3 + k, ((got_c.at[k], nat_c),), natural_c())
            late[k].begin()

        def make_last(h):
            moved = got_c.at[2, halves[h]]
            arrived(moved, z_recv.at[2 + h])
            product_half(5, h, ((moved, nat_c),), natural_c())
            last[h].begin()

        make_a(0)
        make_a(1)
        make_c(0)
        make_a(2)
        norm_y()
        early[0].across()
        for k in range(1, 3):
            early[k].middle(1)
        make_c(1)
        late[0].across()
        make_last(0)
        for k in range(1, 3):
            early[k].middle(2)
        make_last(1)
        late[1].across()
        norm_end(passed)
        last[0].across()
        for k in range(1, 3):
            early[k].middle(3)
        last[1].across()
        for k in range(1, 3):
            early[k].across()
        wait_sends([passed], to_b, nx, ny, late[0].sends, late[1].sends)
        arrived(scale.at[1], n_recv.at[10])
        early[0].end()
        early[1].end()
        direct = lambda k: jnp.where(own_first, F32(0), res[k])
        turned = lambda k: jnp.where(own_first, res[k], F32(0))
        finish_early(direct, turned)
        early[2].end()
        finish(direct, turned)
        wait_sends(*(tile.sends for tile in early + last))


def on_device(greens, pairs, onsets):
    rows, width = greens.shape
    half, cols = rows // 2, width // 3
    vmem = pltpu.VMEM
    dma = pltpu.SemaphoreType.DMA
    return pl.pallas_call(
        kernel,
        out_shape=jax.ShapeDtypeStruct((1, width // (NX * NY), width), F32),
        in_specs=[
            pl.BlockSpec(memory_space=pl.ANY),
            pl.BlockSpec(memory_space=pltpu.SMEM),
            pl.BlockSpec(memory_space=pltpu.SMEM),
        ],
        out_specs=pl.BlockSpec(memory_space=vmem),
        scratch_shapes=[
            vmem((rows, width), BF16),
            vmem((rows, width), BF16),
            vmem((half, width), BF16),
            vmem((3, 2, cols, half), BF16),
            vmem((3, 2, cols, half), BF16),
            vmem((3, cols, half), BF16),
            vmem((3, cols, width), BF16),
            vmem((cols, width), F32),
            vmem((width, cols), F32),
            vmem((6, NX, 64, width), F32),
            vmem((6, NX - 1, 64, width), F32),
            vmem((3, 2, 2, 8, width), F32),
            vmem((3, 3, 2, 4, 8, width), F32),
            vmem((6, 8, 8, width), F32),
            vmem((6, 8, 8, width), F32),
            vmem((6, 8, width), F32),
            vmem((24, width), F32),
            vmem((2, 1, width), F32),
            vmem((NX - 1, 1, width), F32),
            vmem((NY - 1, 1, width), F32),
            vmem((2, 1, width), F32),
            vmem((8, 128), F32),
            vmem((8, 128), F32),
            dma((4,)),
            dma((4,)),
            dma((4,)),
            dma((3, 2)),
            dma((3, 2)),
            dma((96,)),
            dma((96,)),
            dma((32,)),
            dma((11,)),
            dma((11,)),
            dma,
            dma,
        ],
        compiler_params=pltpu.CompilerParams(
            collective_id=0, has_side_effects=True, vmem_limit_bytes=56 * 1024 * 1024
        ),
        cost_estimate=pl.CostEstimate(flops=5_000_000_000, bytes_accessed=4_000_000, transcendentals=768),
    )(greens, pairs, onsets)


def solution(mesh):
    split = Mesh(mesh.devices.reshape(NZ, 2, NX, NY), ("z", "c", "x", "y"))
    in_specs = (P(("x", "y"), ("z", "c")), P(("z", "c"), None), P())
    out_specs = P(("z", "c"), ("x", "y"), None)
    return jax.shard_map(on_device, mesh=split, in_specs=in_specs, out_specs=out_specs, check_vma=False)
```

```python
import functools

import jax
import jax.numpy as jnp
from jax import lax
from jax.experimental import pallas as pl
from jax.experimental.pallas import tpu as pltpu
from jax.sharding import Mesh
from jax.sharding import PartitionSpec as P

MESH = pl.DeviceIdType.MESH
F32 = jnp.float32
BF16 = jnp.bfloat16
NZ, NX, NY = 8, 4, 8
FAR_FIRST = (4, 3, 5, 2, 6, 1, 7)


def remote(src, dst, send, recv, **where):
    return pltpu.make_async_remote_copy(
        src_ref=src, dst_ref=dst, send_sem=send, recv_sem=recv, device_id=where, device_id_type=MESH
    )


def kernel(
    greens, pairs, onsets, out,
    held, nat, nat_c, sent, got, got_c, shift, tbuf, nbuf, units, rx_got, ry_half, ry_full,
    wide, w_got, res, both, npart, nx_got, ny_got, scale, flag, flag_c,
    load_sem, z_send, z_recv, core_send, a_recv, sum_send, sum_recv, own_recv,
    n_send, n_recv, f_send, f_recv,
):
    z, c, x, y = (lax.axis_index(a) for a in ("z", "c", "x", "y"))
    rows, width = greens.shape
    half = rows // 2
    cols = width // 3
    t = x * NY + y
    row_start = t * rows
    z_up, z_down = lax.rem(z + 1, NZ), lax.rem(z + NZ - 1, NZ)
    own = 2 * z + c
    low = lax.rem(own + 2 * NZ - 1, 2 * NZ)
    high = lax.rem(own + 1, 2 * NZ)

    def at_x(d):
        return lax.rem(x + d + NX, NX)

    def at_y(d):
        return lax.rem(y + d + NY, NY)

    bar = pltpu.get_barrier_semaphore()

    def hello(**where):
        pl.semaphore_signal(bar, inc=1, device_id=where, device_id_type=MESH)

    loads = [
        pltpu.make_async_copy(
            greens.at[pl.ds(i * 512, 512)], held.at[pl.ds(i * 512, 512)], load_sem.at[i]
        )
        for i in range(rows // 512)
    ]
    for i in (2, 3, 0, 1):
        pl.when(c == 0)(loads[i].start)
    for i in (0, 1, 2, 3):
        pl.when(c == 1)(loads[i].start)
    hello(c=1 - c)

    @pl.when(c == 0)
    def _():
        hello(z=z_down, c=1)
        for d in range(NY):
            if d:
                hello(z=z_down, y=at_y(d), c=1)

    @pl.when(c == 1)
    def _():
        hello(z=z_up, c=0)
        for d in range(NY):
            if d:
                hello(z=z_up, y=at_y(d), c=0)

    for d in range(1, NX):
        hello(x=at_x(d))
    for d in range(1, NY):
        hello(y=at_y(d))

    for k in range(3):
        i = lax.broadcasted_iota(jnp.int32, (cols, width), 0)
        j = lax.broadcasted_iota(jnp.int32, (cols, width), 1)
        if k < 2:
            hit = j == i + 16 * lax.shift_right_logical(i, 3) + 8 * k
        else:
            h, rest = lax.shift_right_logical(i, 7), i & 127
            hit = j == rest + 20 * lax.shift_right_logical(rest, 2) + 16 + 4 * h
        shift[k] = jnp.where(hit, F32(1), F32(0)).astype(BF16)

    own_first = pairs[0, 0] == own
    flag[...] = jnp.where(own_first, jnp.ones_like(flag), jnp.zeros_like(flag))

    def chunk(k, h):
        for b in range(2):
            part = held[pl.ds(h * half + b * 512, 512), :]
            sent[k, h, :, pl.ds(b * 512, 512)] = lax.dot_general(
                shift[k], part, (((1,), (1,)), ((), ())), preferred_element_type=F32
            ).astype(BF16)

    def masks(first, last, targets, total):
        own_from = onsets[own] - row_start
        step = 64

        def body(i, total):
            at = pl.multiple_of(i * step, step)
            block = held[pl.ds(at, step), :].astype(F32)
            ids = at + lax.broadcasted_iota(jnp.int32, (step, width), 0)
            for ref, shifted, onset in targets:
                to = pl.multiple_of(at - shifted, step)
                ref[pl.ds(to, step), :] = jnp.where(ids >= onset - row_start, block, F32(0)).astype(BF16)
            mine = jnp.where(ids >= own_from, block, F32(0))
            return total + jnp.sum((mine * mine).reshape(step // 8, 8, width), axis=0)

        return lax.fori_loop(first // step, last // step, body, total)

    nx = [
        remote(npart.at[0], nx_got.at[d - 1], n_send.at[d - 1], n_recv.at[d - 1], x=at_x(d))
        for d in range(1, NX)
    ]
    ny = [
        remote(npart.at[1], ny_got.at[d - 1], n_send.at[2 + d], n_recv.at[2 + d], y=at_y(d))
        for d in range(1, NY)
    ]

    def norm_x(total):
        npart[0] = jnp.sum(total, axis=0, keepdims=True)
        for cp in nx:
            cp.start()

    def norm_y():
        total = npart[0]
        for d, cp in enumerate(nx):
            cp.wait_recv()
            total = total + nx_got[d]
        npart[1] = total
        for cp in ny:
            cp.start()

    def norm_end(pass_on):
        total = npart[1]
        for d, cp in enumerate(ny):
            cp.wait_recv()
            total = total + ny_got[d]
        scale[0] = lax.rsqrt(total + F32(1e-6))
        pass_on.start()

    def product(u, parts, natural):
        for q in range(3):
            at = pl.ds(q * cols, cols)
            total = None
            for moved, still in parts:
                term = jnp.dot(moved[...], still[:, at], preferred_element_type=F32)
                total = term if total is None else total + term
            tbuf[:, at] = total
            nbuf[at, :] = total.T
        for g in range(NX):
            turned = nbuf[pl.ds(192 * g, 192), :].reshape(8, 3, 8, cols)
            for q in range(3):
                at = pl.ds(q * cols, cols)
                plain = tbuf[pl.ds(64 * g, 64), at]
                units[u, g, :, at] = jnp.where(natural, turned[:, q].reshape(64, cols), plain)

    def product_half(u, h, parts, natural):
        total = None
        for moved, still in parts:
            term = jnp.dot(moved[...], still[...], preferred_element_type=F32)
            total = term if total is None else total + term
        half_cols, few = width // 2, cols // 2
        nbuf[:, pl.ds(0, few)] = total.T
        left, right = total[:, :half_cols], total[:, half_cols:]
        top = lax.broadcasted_iota(jnp.int32, (few, half_cols), 0) & 7 < 4
        even = jnp.where(top, left, pltpu.roll(right, 4, 0)).reshape(16, 1, 8, half_cols)
        odd = jnp.where(top, pltpu.roll(left, few - 4, 0), right).reshape(16, 1, 8, half_cols)
        tbuf[:, pl.ds(0, half_cols)] = jnp.concatenate([even, odd], axis=1).reshape(cols, half_cols)
        for g in range(NX):
            turned = nbuf[pl.ds(192 * g, 192), pl.ds(0, few)].reshape(8, 3, 8, few)
            for q in range(3):
                plain = tbuf[pl.ds(64 * g, 64), pl.ds(q * few, few)]
                to = pl.ds(h * half_cols + q * few, few)
                units[u, g, :, to] = jnp.where(natural[:, :few], turned[:, q].reshape(64, few), plain)

    def arrived(ref, sem):
        pltpu.make_async_copy(ref, ref, sem).wait()

    class Chunk:
        def __init__(self, u, slot, first=0, count=None, away=None):
            self.u, self.away, self.sends, self.base = u, away, [], 12 * slot
            self.cut = pl.ds(first, width if count is None else count)

        def go(self, index, src, dst, sem=None, **where):
            at = self.base + index
            cp = remote(src, dst, sum_send.at[at], sum_recv.at[at] if sem is None else sem, **where)
            cp.start()
            self.sends.append(cp)

        def y_rows(self, g):
            return units.at[self.u, :, pl.ds(pl.multiple_of(8 * g, 8), 8), self.cut]

        def x_ends(self):
            for d in range(1, NX):
                self.go(7 + d, wide.at[self.u, at_x(d), :, self.cut], w_got.at[self.u, d, :, self.cut], x=at_x(d))

        def end(self):
            total = wide[self.u, x, :, self.cut]
            for d in range(1, NX):
                self.sends[-NX + d].wait_recv()
                total = total + w_got[self.u, d, :, self.cut]
            res[self.u, :, self.cut] = total

    class RingY(Chunk):
        def slot(self, step, side):
            return ry_half.at[self.u, side] if step == 0 else ry_full.at[self.u, step - 1, side]

        def both(self, step, srcs):
            for side in range(2):
                self.go(2 * step + side, srcs[side], self.slot(step, side), y=at_y(1 - 2 * side))

        def begin(self):
            far = self.y_rows(at_y(NY // 2))
            self.both(0, [far.at[pl.ds(2 * side, 2)] for side in range(2)])

        def middle(self, step):
            last = self.sends[-2:]
            for side in range(2):
                last[side].wait_recv()
                where = self.y_rows(at_y((NY // 2 - step) * (1 - 2 * side)))
                if step == 1:
                    where = where.at[pl.ds(2 * side, 2)]
                where[...] = where[...] + self.slot(step - 1, side)[...]
            self.both(step, [self.y_rows(at_y((NY // 2 - step) * (1 - 2 * side))) for side in range(2)])

        def across(self):
            for cp in self.sends[-2:]:
                cp.wait_recv()
            deep = NY // 2 - 1
            wide[self.u, pl.ds(0, 4)] = self.y_rows(y)[...] + self.slot(deep, 0)[...] + self.slot(deep, 1)[...]
            self.x_ends()

    class AllX(Chunk):
        def begin(self):
            for d in (2, 1, 3):
                self.go(
                    d, units.at[self.u, at_x(d), :, self.cut], rx_got.at[self.u, d - 1, :, self.cut], x=at_x(d)
                )

        def across(self):
            total = units[self.u, x, :, self.cut]
            for i, d in enumerate((2, 1, 3)):
                self.sends[i].wait_recv()
                total = total + rx_got[self.u, d - 1, :, self.cut]
            wide[self.u, :, :, self.cut] = total.reshape(8, 8, -1)
            for d in FAR_FIRST + ((0,) if self.away is not None else ()):
                src, dst = wide.at[self.u, at_y(d), :, self.cut], w_got.at[self.u, d, :, self.cut]
                if self.away is None:
                    self.go(4 + d, src, dst, y=at_y(d))
                else:
                    self.go(4 + d, src, dst, own_recv.at[8 * self.away + d], z=z_up, c=0, y=at_y(d))

        def end(self):
            total = wide[self.u, y, :, self.cut]
            for i, d in enumerate(FAR_FIRST):
                self.sends[3 + i].wait_recv()
                total = total + w_got[self.u, d, :, self.cut]
            res[self.u, :, self.cut] = total

    def end_c(k, away, first=0, count=None):
        total = None
        cut = pl.ds(first, width if count is None else count)
        for d in range(NY):
            arrived(w_got.at[3 + k, d, :, cut], own_recv.at[8 * away + d])
            total = w_got[3 + k, d, :, cut] if total is None else total + w_got[3 + k, d, :, cut]
        res[3 + k, :, cut] = total

    def put_back(piece, k):
        top = piece.astype(BF16).astype(F32)
        rest = piece - top
        mid = rest.astype(BF16).astype(F32)
        stack = jnp.concatenate([top, mid, rest - mid], axis=0).astype(BF16)
        total = jnp.dot(stack, shift[k], preferred_element_type=F32)
        return total[:24] + total[24:48] + total[48:]

    def finish_early(direct, turned):
        total = None
        for k in range(2):
            piece = turned(k)
            piece = jnp.concatenate([piece[:, q * cols : (q + 1) * cols] for q in range(3)], axis=0)
            term = put_back(piece, k)
            total = term if total is None else total + term
        out[0] = total
        for k in range(2):
            out[0, pl.ds(8 * k, 8), :] = out[0, pl.ds(8 * k, 8), :] + direct(k)
        mine, other = scale[0], scale[1]
        left = jnp.where(own_first, mine, other)
        right = jnp.where(own_first, other, mine)
        i = lax.broadcasted_iota(jnp.int32, (24, width), 0)
        j = lax.broadcasted_iota(jnp.int32, (24, width), 1)
        down = jnp.sum(jnp.where(j == i + 24 * t, left, F32(0)), axis=1, keepdims=True)
        both[...] = down * right

    def finish(direct, turned):
        few, half_cols = cols // 2, width // 2
        piece = turned(2)
        piece = jnp.concatenate(
            [
                jnp.concatenate([piece[:, h * half_cols + q * few : h * half_cols + (q + 1) * few] for q in range(3)], axis=0)
                for h in range(2)
            ],
            axis=1,
        )
        value = out[0] + put_back(piece, 2)
        straight = direct(2)
        low_half, high_half = straight[:, :half_cols], straight[:, half_cols:]
        top = lax.broadcasted_iota(jnp.int32, (8, half_cols), 0) < 4
        straight = jnp.concatenate(
            [
                jnp.where(top, low_half, pltpu.roll(high_half, 4, 0)),
                jnp.where(top, pltpu.roll(low_half, 4, 0), high_half),
            ],
            axis=1,
        )
        out[0, pl.ds(0, 16), :] = value[:16] * both[pl.ds(0, 16), :]
        out[0, pl.ds(16, 8), :] = (value[16:] + straight) * both[pl.ds(16, 8), :]

    def wait_sends(*groups):
        for group in groups:
            for cp in group:
                cp.wait_send()

    whole, halves = pl.ds(0, cols), [pl.ds(cols // 2 * h, cols // 2) for h in range(2)]
    pieces = [(0, whole), (1, whole), (2, halves[0]), (2, halves[1])]
    half_width = width // 2
    nothing = jnp.zeros((8, width), F32)
    first_rows, last_rows = pl.ds(0, half), pl.ds(half, half)

    @pl.when(c == 0)
    def _():
        flags = remote(flag, flag_c, f_send, f_recv, z=z_down, c=1)
        to_c = [
            remote(sent.at[k, 1, r], got_c.at[k, r], z_send.at[i], z_recv.at[i], z=z_down, c=1)
            for i, (k, r) in enumerate(pieces)
        ]
        to_a = [
            [remote(sent.at[k, h], got.at[k, h], core_send.at[k, h], a_recv.at[k, h], c=1) for h in range(2)]
            for k in range(3)
        ]
        passed = remote(scale.at[0], scale.at[1], n_send.at[10], n_recv.at[10], c=1)
        for i in (2, 3):
            loads[i].wait()
        chunk(0, 1)
        pl.semaphore_wait(bar, NX + NY - 1 + NY)
        to_c[0].start()
        to_a[0][1].start()
        flags.start()
        for i in (0, 1):
            loads[i].wait()
        for k in range(3):
            if k:
                chunk(k, 1)
                to_c[k].start()
                if k == 2:
                    to_c[3].start()
                to_a[k][1].start()
            chunk(k, 0)
            to_a[k][0].start()
        total = masks(0, half, [(nat, 0, jnp.maximum(onsets[own], onsets[low]))], nothing)
        norm_x(masks(half, rows, [], total))

        tiles = [RingY(0, 0), RingY(1, 1)]
        last = [AllX(2, 2, 0, half_width), AllX(2, 6, half_width, half_width)]

        def make(k):
            arrived(got.at[k, 0], z_recv.at[k])
            product(k, ((got.at[k, 0], nat.at[first_rows]),), own_first)
            tiles[k].begin()

        def make_last(h):
            moved = got.at[2, 0, halves[h]]
            arrived(moved, z_recv.at[2 + h])
            product_half(2, h, ((moved, nat.at[first_rows]),), jnp.broadcast_to(own_first, (64, cols)))
            last[h].begin()

        make(0)
        norm_y()
        tiles[0].middle(1)
        make(1)
        make_last(0)
        tiles[0].middle(2)
        make_last(1)
        tiles[1].middle(1)
        norm_end(passed)
        tiles[0].middle(3)
        tiles[1].middle(2)
        last[0].across()
        tiles[0].across()
        tiles[1].middle(3)
        last[1].across()
        tiles[0].end()
        end_c(0, 0)
        tiles[1].across()
        wait_sends([flags, passed], to_c, nx, ny, *to_a, tiles[0].sends)
        arrived(scale.at[1], n_recv.at[10])
        end_c(1, 1)
        tiles[1].end()
        direct = lambda k: jnp.where(own_first, res[3 + k], res[k])
        turned = lambda k: jnp.where(own_first, res[k], res[3 + k])
        finish_early(direct, turned)
        wait_sends(tiles[1].sends)
        for h in range(2):
            last[h].end()
            end_c(2, 2 + h, half_width * h, half_width)
        finish(direct, turned)
        wait_sends(last[0].sends, last[1].sends)

    @pl.when(c == 1)
    def _():
        to_b = [
            remote(sent.at[k, 0, r], got.at[k, 0, r], z_send.at[i], z_recv.at[i], z=z_up, c=0)
            for i, (k, r) in enumerate(pieces)
        ]
        passed = remote(scale.at[0], scale.at[1], n_send.at[10], n_recv.at[10], z=z_up, c=0)
        for i in (0, 1):
            loads[i].wait()
        chunk(0, 0)
        pl.semaphore_wait(bar, NX + NY - 1 + NY)
        to_b[0].start()
        for k in (1, 2):
            chunk(k, 0)
            to_b[k].start()
        to_b[3].start()
        for i in (2, 3):
            loads[i].wait()
        onset_a = jnp.maximum(onsets[own], onsets[low])
        onset_c = jnp.maximum(onsets[own], onsets[high])
        total = masks(0, half, [(nat, 0, onset_a)], nothing)
        norm_x(masks(half, rows, [(nat, 0, onset_a), (nat_c, half, onset_c)], total))

        early = [AllX(0, 0), RingY(1, 1), RingY(2, 2)]
        late = [AllX(3, 3, away=0), AllX(4, 4, away=1)]
        last = [AllX(5, 5, 0, half_width, 2), AllX(5, 7, half_width, half_width, 3)]

        def make_a(k):
            for h in range(2):
                arrived(got.at[k, h], a_recv.at[k, h])
            if k < 2:
                product(k, ((got.at[k, 0], nat.at[first_rows]), (got.at[k, 1], nat.at[last_rows])), own_first)
            else:
                for h in range(2):
                    parts = ((got.at[2, 0, halves[h]], nat.at[first_rows]), (got.at[2, 1, halves[h]], nat.at[last_rows]))
                    product_half(2, h, parts, jnp.broadcast_to(own_first, (64, cols)))
            early[k].begin()

        def natural_c():
            return jnp.broadcast_to(flag_c[0:1, 0:1] < F32(0.5), (64, cols))

        def make_c(k):
            if k == 0:
                arrived(flag_c, f_recv)
            arrived(got_c.at[k], z_recv.at[k])
            product(3 + k, ((got_c.at[k], nat_c),), natural_c())
            late[k].begin()

        def make_last(h):
            moved = got_c.at[2, halves[h]]
            arrived(moved, z_recv.at[2 + h])
            product_half(5, h, ((moved, nat_c),), natural_c())
            last[h].begin()

        make_a(0)
        make_a(1)
        make_c(0)
        make_a(2)
        norm_y()
        early[1].middle(1)
        early[0].across()
        make_c(1)
        early[2].middle(1)
        make_last(0)
        late[0].across()
        early[1].middle(2)
        make_last(1)
        early[2].middle(2)
        late[1].across()
        norm_end(passed)
        last[0].across()
        for k in range(1, 3):
            early[k].middle(3)
        last[1].across()
        for k in range(1, 3):
            early[k].across()
        wait_sends([passed], to_b, nx, ny, late[0].sends, late[1].sends)
        arrived(scale.at[1], n_recv.at[10])
        early[0].end()
        early[1].end()
        direct = lambda k: jnp.where(own_first, F32(0), res[k])
        turned = lambda k: jnp.where(own_first, res[k], F32(0))
        finish_early(direct, turned)
        early[2].end()
        finish(direct, turned)
        wait_sends(*(tile.sends for tile in early + last))


def on_device(greens, pairs, onsets):
    rows, width = greens.shape
    half, cols = rows // 2, width // 3
    vmem = pltpu.VMEM
    dma = pltpu.SemaphoreType.DMA
    return pl.pallas_call(
        kernel,
        out_shape=jax.ShapeDtypeStruct((1, width // (NX * NY), width), F32),
        in_specs=[
            pl.BlockSpec(memory_space=pl.ANY),
            pl.BlockSpec(memory_space=pltpu.SMEM),
            pl.BlockSpec(memory_space=pltpu.SMEM),
        ],
        out_specs=pl.BlockSpec(memory_space=vmem),
        scratch_shapes=[
            vmem((rows, width), BF16),
            vmem((rows, width), BF16),
            vmem((half, width), BF16),
            vmem((3, 2, cols, half), BF16),
            vmem((3, 2, cols, half), BF16),
            vmem((3, cols, half), BF16),
            vmem((3, cols, width), BF16),
            vmem((cols, width), F32),
            vmem((width, cols), F32),
            vmem((6, NX, 64, width), F32),
            vmem((6, NX - 1, 64, width), F32),
            vmem((3, 2, 2, 8, width), F32),
            vmem((3, 3, 2, 4, 8, width), F32),
            vmem((6, 8, 8, width), F32),
            vmem((6, 8, 8, width), F32),
            vmem((6, 8, width), F32),
            vmem((24, width), F32),
            vmem((2, 1, width), F32),
            vmem((NX - 1, 1, width), F32),
            vmem((NY - 1, 1, width), F32),
            vmem((2, 1, width), F32),
            vmem((8, 128), F32),
            vmem((8, 128), F32),
            dma((4,)),
            dma((4,)),
            dma((4,)),
            dma((3, 2)),
            dma((3, 2)),
            dma((96,)),
            dma((96,)),
            dma((32,)),
            dma((11,)),
            dma((11,)),
            dma,
            dma,
        ],
        compiler_params=pltpu.CompilerParams(
            collective_id=0, has_side_effects=True, vmem_limit_bytes=56 * 1024 * 1024
        ),
        cost_estimate=pl.CostEstimate(flops=5_000_000_000, bytes_accessed=4_000_000, transcendentals=768),
    )(greens, pairs, onsets)


def solution(mesh):
    split = Mesh(mesh.devices.reshape(NZ, 2, NX, NY), ("z", "c", "x", "y"))
    in_specs = (P(("x", "y"), ("z", "c")), P(("z", "c"), None), P())
    out_specs = P(("z", "c"), ("x", "y"), None)
    return jax.shard_map(on_device, mesh=split, in_specs=in_specs, out_specs=out_specs, check_vma=False)
```
